32 devices in a mesh: tm: 16 (over z, y, x), pad: 2 (over core).
Axes of the slice: x: 2, y: 2, z: 4, core: 2. Of those that a mesh axis runs over, the one named last changes fastest.
Arguments:
- charge: float32 [2, 8192], P('pad', 'tm'), may hold values from 0.3 to 3
- pad_row: int32 [2, 8192], P('pad', 'tm'), may hold values from 0 to 39
- pad_column: int32 [2, 8192], P('pad', 'tm'), may hold values from 0 to 65
- time_bin: int32 [2, 8192], P('pad', 'tm'), may hold values from 0 to 1023
- slab_owner: int32 [2, 8192, 1], P('pad', 'tm'), may hold values from 0 to 15; in each aligned block of 512 rows (0 to 511, 512 to 1023, ..., all dimensions but the last counted through in order) at most 48 rows name the same one
- block_count: int32 [2, 64], P('pad', 'tm'), may hold values from 1 to 128
- shaping: float32 [1024], replicated, may hold values from 0.02 to 1
- response: float32 [3, 3], replicated, may hold values from 0.05 to 1
Outputs:
- signal: float32 [80, 66, 16384], P('pad', None, 'tm')
The draws below stay inside these ranges and needn't reach their ends.
Inputs may be any that keep to these rules, and one draw needn't show every extreme that they name: `slab_owner`: among the cluster rows of one device, at most 48 name the same time slab, a bound that some of them reach. Only the first block_count rows of each block of 128 cluster rows hold clusters.
All inputs are finite; a program needn't handle non-finite values.
Results may differ from the reference program's by a relative error of at most 0.0003.
Values sent between devices are 32-bit elements; how exact they have to be, the bound alone decides.
No kernel may reach another device: no remote copies, remote signals or barrier semaphores. Data moves between devices by JAX's collectives and lax.ppermute only.
A program may use at most 128 MiB of HBM per device.

```python
import math
import jax
import jax.numpy as jnp
import numpy as np
from jax import lax

PROWS = 80
PPR = 66
T_DEV = 1024
KLEN = 1024
SRC_ROWS = 512
CAP = 48
SRC_ALL = 8192
BLK_ALL = 64
RG = 40
N_TM = 16
N_PAD = 2


def with_ends(entries, rng, smallest, high):
    dims = entries.shape
    index_at = [jax.random.randint(jax.random.fold_in(rng, axis), (), 0, dims[axis]) for axis in range(len(dims))]
    entries = entries.at[tuple(index_at)].set(smallest)
    longest = dims.index(max(dims))
    index_at[longest] = (index_at[longest] + 1) % dims[longest]
    return entries.at[tuple(index_at)].set(high)


def levels(stream_key, extent, cuts, least, top_value):
    def one(dim, shards_of):
        steps = jax.random.uniform(jax.random.fold_in(jax.random.fold_in(stream_key, 6), dim), (shards_of,), jnp.float32, least / len(cuts), top_value / len(cuts))
        return jnp.repeat(jnp.exp(steps), extent[dim] // shards_of).reshape((-1,) + (1,) * (len(extent) - dim - 1))

    factor_of = one(*cuts[0])
    for cut in cuts[1:]:
        factor_of = factor_of * one(*cut)
    return factor_of


def assign_block(stream_key, own, number, rows, number_of, top, most, skew):
    sequence = jax.random.permutation(stream_key, number_of)
    packed, usual = load_shares(number_of, rows * top, most, skew, True), load_shares(number_of, rows * top, most, skew, False)
    places = jnp.arange(number_of)

    def named(tallies, offset_by):
        used = int((tallies > 0).sum())
        fixed = max(1, used // 4)
        passed = fixed + (places - fixed + offset_by * (used - fixed)) % max(1, number_of - fixed)
        return jnp.zeros((number_of,), jnp.int32).at[sequence[jnp.where(places < fixed, places, passed)]].set(jnp.asarray(tallies, jnp.int32))

    tallies = jnp.where(number % 4 == 0, named(packed, number // 4), named(usual, number - number // 4 - 1))
    mixed = jax.random.permutation(jax.random.fold_in(own, 3), number_of)
    source_of, sink = mixed[0:number_of // 2 * 2:2], mixed[1:number_of // 2 * 2:2]
    slack = jnp.minimum(tallies[source_of] - 1, most - tallies[sink]) // 2
    slack = jnp.where((source_of == sequence[0]) | (sink == sequence[0]) | (tallies[sink] == 0), 0, jnp.maximum(slack, 0))
    passed = jax.random.randint(jax.random.fold_in(own, 4), (number_of // 2,), 0, 1 << 20) % (slack + 1)
    tallies = tallies.at[source_of].add(-passed).at[sink].add(passed)
    labels = jnp.searchsorted(jnp.cumsum(tallies), jnp.arange(rows * top), side="right").astype(jnp.int32)
    table = labels.reshape(top, rows).T
    table = table[jax.random.permutation(jax.random.fold_in(own, 1), rows)]
    offset_by = jax.random.randint(jax.random.fold_in(own, 2), (rows, 1), 0, top)
    return jnp.take_along_axis(table, (jnp.arange(top)[None, :] + offset_by) % top, axis=1)


def load_shares(count, total, reach, slope, full):
    portions = [(1 << 20) // math.isqrt(grade ** slope) + 1 for grade in range(1, count + 1)]
    largest = reach if full else min(reach, max(-(-total // count), total * portions[0] // sum(portions)))
    least = 1 if total - largest >= count - 1 else 0
    holding, spare = [largest] + [least] * (count - 1), total - largest - least * (count - 1)
    while spare > 0:
        candidates = [i for i in range(1, count) if holding[i] < largest] or [i for i in range(1, count) if holding[i] < reach]
        whole, left = sum([portions[i] for i in candidates]), spare
        for i in candidates:
            extra = min(reach - holding[i], max(1, left * portions[i] // whole), spare)
            holding[i] = holding[i] + extra
            spare = spare - extra
    return np.array(holding)


def setup_inputs(seed: int = 0) -> dict:
    streams_of = jax.random.split(jax.random.key(seed), 9)
    charge = jnp.clip(jnp.exp(math.log(3.0) - 2.3025851 * jax.random.uniform(streams_of[0], (N_PAD, SRC_ALL), jnp.float32) ** levels(streams_of[0], (N_PAD, SRC_ALL), ((0, 2), (1, 16)), -0.2, 0.2)), 0.3, 3.0)
    pad_row = with_ends(jax.random.randint(streams_of[1], (N_PAD, SRC_ALL), 0, RG), jax.random.fold_in(streams_of[1], 1), 0, RG - 1).astype(jnp.int32)
    pad_column = with_ends(jax.random.randint(streams_of[2], (N_PAD, SRC_ALL), 0, PPR), jax.random.fold_in(streams_of[2], 1), 0, PPR - 1).astype(jnp.int32)
    time_bin = with_ends(jax.random.randint(streams_of[3], (N_PAD, SRC_ALL), 0, T_DEV), jax.random.fold_in(streams_of[3], 1), 0, T_DEV - 1).astype(jnp.int32)
    slab_owner_keys = jax.random.split(jax.random.fold_in(streams_of[4], 1), N_PAD * SRC_ALL // SRC_ROWS)
    slab_owner_turns = jax.random.permutation(jax.random.fold_in(streams_of[4], 3), N_PAD * SRC_ALL // SRC_ROWS)
    slab_owner = jax.vmap(lambda own, number: assign_block(jax.random.fold_in(streams_of[4], 2), own, number, SRC_ROWS, N_TM, 1, CAP, 2))(slab_owner_keys, slab_owner_turns).reshape((N_PAD, SRC_ALL, 1))
    block_count = with_ends(jax.random.randint(streams_of[5], (N_PAD, BLK_ALL), 1, 129), jax.random.fold_in(streams_of[5], 1), 1, 128).astype(jnp.int32)
    shaping = jnp.clip(jax.random.uniform(streams_of[6], (KLEN,), jnp.float32, 0.02, 1.0), 0.02, 1.0)
    response = jnp.clip(jax.random.uniform(streams_of[7], (3, 3), jnp.float32, 0.05, 1.0), 0.05, 1.0)
    return dict(charge=charge, pad_row=pad_row, pad_column=pad_column, time_bin=time_bin, slab_owner=slab_owner, block_count=block_count, shaping=shaping, response=response)


def lag_tables(shaping):
    width = 128
    count = shaping.shape[0] // width + 1
    longer = jnp.concatenate([jnp.zeros((width,), shaping.dtype), shaping, jnp.zeros((2 * width,), shaping.dtype)])
    tables = []
    for lag_block in range(count):
        base = width + width * lag_block
        line = jnp.concatenate([longer[base:base + width], jnp.zeros((1,), shaping.dtype), longer[base - width + 1:base]])
        tiled = jnp.tile(line, width)[: width * (2 * width - 1)].reshape(width, 2 * width - 1)
        tables.append(tiled[:, :width])
    return tables


def shape_time(current, previous, tables):
    cells, bins = current.shape
    blocks = bins // 128
    extended = jnp.concatenate([previous.reshape(cells, blocks, 128), current.reshape(cells, blocks, 128)], axis=1)
    result = jnp.zeros((cells * blocks, 128), current.dtype)
    for lag_block, table in enumerate(tables):
        piece = extended[:, blocks - lag_block:2 * blocks - lag_block].reshape(cells * blocks, 128)
        result = result + jnp.dot(piece, table, precision=lax.Precision.HIGHEST, preferred_element_type=current.dtype)
    return result.reshape(cells, bins)


def spread(padded, response):
    row_count = padded.shape[0] - 2
    columns = padded.shape[1]
    wide = jnp.pad(padded, ((0, 0), (1, 1), (0, 0)))
    result = jnp.zeros((row_count, columns, padded.shape[2]), padded.dtype)
    for above in range(3):
        for beside in range(3):
            result = result + response[above, beside] * wide[above:above + row_count, beside:beside + columns]
    return result


def reference(charge, pad_row, pad_column, time_bin, slab_owner, block_count, shaping, response):
    cells = (PROWS // N_PAD) * PPR
    bins = T_DEV * N_TM
    tables = lag_tables(shaping)

    def one_group(group):
        charge_g, row_g, column_g, bin_g, owner_g, count_g = group
        total = charge_g.shape[0]
        live = (lax.broadcasted_iota(jnp.int32, (total // 128, 128), 1) < count_g[:, None]).reshape(total)
        cell = (row_g * PPR + column_g).astype(jnp.int32)
        moment = (owner_g * T_DEV + bin_g).astype(jnp.int32)
        grid = jnp.zeros((cells, bins), charge_g.dtype).at[cell, moment].add(jnp.where(live, charge_g, 0.0))
        return shape_time(grid, jnp.zeros_like(grid), tables)

    shaped = lax.map(one_group, (charge, pad_row, pad_column, time_bin, slab_owner[:, :, 0], block_count))
    shaped = shaped.reshape(PROWS, PPR, bins)
    padded = jnp.pad(shaped, ((1, 1), (0, 0), (0, 0)))
    return spread(padded, response)
```

```python
import functools

import jax
import jax.numpy as jnp
from jax import lax
from jax.experimental import pallas as pl
from jax.experimental.pallas import tpu as pltpu
from jax.sharding import PartitionSpec as P

PROWS = 80
PPR = 66
T_DEV = 1024

LANES = 128
GROUP = 6
WINDOW = 80
NT = (((1,), (1,)), ((), ()))


def iota(shape, dim):
    return lax.broadcasted_iota(jnp.int32, shape, dim)


def pieces(x):
    high = x.astype(jnp.bfloat16).astype(jnp.float32)
    rest = x - high
    middle = rest.astype(jnp.bfloat16).astype(jnp.float32)
    low = rest - middle
    return jnp.concatenate([high, middle, low, jnp.zeros_like(x)], axis=0).astype(jnp.bfloat16)


def joined(x):
    return (x[0:4] + x[4:8]) + x[8:12]


def running():
    source, lane = iota((LANES, 2 * LANES), 0), iota((LANES, 2 * LANES), 1)
    return jnp.where((lane >= LANES) | (source <= lane), 1.0, 0.0).astype(jnp.bfloat16)


def route_kernel(slabs, pads, row_count, room, group_ref, *refs):
    sources, (out_ref,), (sems,), targets = refs[:6], refs[6:7], refs[7:8], refs[8:]
    copies = [pltpu.make_async_copy(*pair, sems.at[k]) for k, pair in enumerate(zip(sources, targets))]
    for copy in copies:
        copy.start()
    for copy in copies:
        copy.wait()
    count_ref, charge_ref, row_ref, column_ref, bin_ref, slab_ref = targets
    rows = charge_ref.shape[1]
    blocks = rows // LANES
    group = group_ref[0]
    sums = running()
    slab_ids = iota((slabs, LANES), 0)
    lane = iota((1, LANES), 1)
    before = jnp.zeros((slabs, LANES), jnp.float32)
    slots, values = [], []
    for block in range(blocks):
        at = pl.ds(block * LANES, LANES)
        live = lane < count_ref[0, block]
        slab = jnp.where(live, slab_ref[:, at], -1)
        marks = jnp.where(slab_ids == slab, 1.0, 0.0)
        totals = jnp.dot(marks.astype(jnp.bfloat16), sums, preferred_element_type=jnp.float32)
        rank = jnp.sum(marks * (totals[:, :LANES] + before), axis=0, keepdims=True)
        before = before + totals[:, LANES:]
        slots.append(jnp.where(live, slab * room + rank.astype(jnp.int32) - 1, -1))
        values.append(
            jnp.concatenate(
                [
                    charge_ref[:, at],
                    (row_ref[:, at] + 2).astype(jnp.float32),
                    column_ref[:, at].astype(jnp.float32),
                    bin_ref[:, at].astype(jnp.float32),
                ],
                axis=0,
            )
        )
    payload = pieces(jnp.concatenate(values, axis=1))
    slot = jnp.concatenate(slots, axis=1)
    hits = jnp.where(iota((slabs * room, rows), 0) == slot, 1.0, 0.0).astype(jnp.bfloat16)
    placed = joined(lax.dot_general(payload, hits, NT, preferred_element_type=jnp.float32))
    feature, half = iota((4, LANES), 0), iota((4, LANES), 1) // room
    for slab in range(slabs):
        tile = placed[:, slab // 2 * LANES : slab // 2 * LANES + LANES]
        if slab % 2 == 0:
            other = placed[:, (slab // 2 - 1) * LANES : slab // 2 * LANES] if slab else jnp.zeros_like(tile)
            tile = jnp.where(half == 0, tile, other)
        tile = jnp.where((feature == 3) & (half != slab % 2), tile - T_DEV, tile)
        top = jnp.where(feature == 1, jnp.where(tile == row_count + 1, 1.0, 0.0), tile)
        bottom = jnp.where(feature == 1, jnp.where(tile == 2, row_count + 2.0, 0.0), tile)
        for pad in range(pads):
            apart = pad - group
            out_ref[slab * pads + pad] = jnp.where(
                apart == 0, tile, jnp.where(apart == 1, top, jnp.where(apart == -1, bottom, 0.0))
            )


def signal_kernel(
    row_count,
    response_ref,
    slots_ref,
    shaping_ref,
    out_ref,
    payload_ref,
    place_ref,
    marks_ref,
    totals_ref,
    table_ref,
    feature_ref,
    time_ref,
    first_ref,
    stage_ref,
    high_ref,
    low_ref,
    result_ref,
    time_smem,
    first_smem,
    time_sem,
    first_sem,
    out_sems,
):
    count = slots_ref.shape[0]
    step = min(count, 32)
    parts = count // step
    buckets = first_ref.shape[0]
    chunks = T_DEV // LANES

    sums = running()
    bucket_ids = iota((buckets, LANES), 0).astype(jnp.float32)

    def mark(part, earlier):
        for k in range(step):
            block = part * step + k
            slot = slots_ref[block]
            payload_ref[block] = pieces(slot)
            column = slot[2:3] + 1.0
            block_at = jnp.floor((column + 0.5) * (1.0 / GROUP))
            inner = jnp.where(column - block_at * GROUP > 1.5, 1.0, 0.0)
            bucket = jnp.where(slot[1:2] > 0.5, 2.0 * block_at + inner, -1.0)
            marks_ref[pl.ds(block * buckets, buckets), :] = jnp.where(bucket_ids == bucket, 1.0, 0.0)
            earlier = earlier + jnp.where((bucket >= 0.0) & (bucket < bucket_ids), 1.0, 0.0)
        return earlier

    earlier = lax.fori_loop(0, parts, mark, jnp.zeros((buckets, LANES), jnp.float32))
    first = jnp.dot(earlier.astype(jnp.bfloat16), sums, preferred_element_type=jnp.float32)[:, LANES:]
    first_ref[...] = first.astype(jnp.int32)
    first_copy = pltpu.make_async_copy(first_ref, first_smem, first_sem)
    first_copy.start()

    def number(part, before):
        at = pl.ds(part * step * buckets, step * buckets)
        totals_ref[...] = jnp.dot(marks_ref[at, :].astype(jnp.bfloat16), sums, preferred_element_type=jnp.float32)
        for k in range(step):
            block = part * step + k
            marks = marks_ref[pl.ds(block * buckets, buckets), :]
            within = totals_ref[k * buckets : (k + 1) * buckets, :LANES]
            place_ref[block] = jnp.sum(marks * (within + before), axis=0, keepdims=True)
            before = before + totals_ref[k * buckets : (k + 1) * buckets, LANES:]
        return before

    lax.fori_loop(0, parts, number, first)
    total = jnp.max(first).astype(jnp.int32)
    filled = (total + LANES - 1) // LANES

    position = iota((LANES, LANES), 0).astype(jnp.float32) + 1.0

    def sort(chunk, carry):
        wanted = position + (chunk * LANES).astype(jnp.float32)

        def add(part, accum):
            hits = [
                jnp.where(place_ref[part * step + k] == wanted, 1.0, 0.0).astype(jnp.bfloat16)
                for k in range(step)
            ]
            held = [payload_ref[part * step + k] for k in range(step)]
            return accum + lax.dot_general(
                jnp.concatenate(held, axis=1),
                jnp.concatenate(hits, axis=1),
                NT,
                preferred_element_type=jnp.float32,
            )

        placed = joined(lax.fori_loop(0, parts, add, jnp.zeros((16, LANES), jnp.float32)))
        feature_ref[chunk] = placed
        time_ref[pl.ds(chunk, 1), :] = placed[3:4].astype(jnp.int32)
        return carry

    lax.fori_loop(0, filled, sort, 0)
    feature_ref[filled] = jnp.zeros((4, LANES), jnp.float32)
    time_copy = pltpu.make_async_copy(time_ref, time_smem, time_sem)
    time_copy.start()

    kernel = shaping_ref[...]
    lane, sublane = iota((chunks, LANES), 1), iota((chunks, LANES), 0)
    moved = jnp.concatenate([jnp.zeros((1, LANES), jnp.float32), kernel[: chunks - 1]], axis=0)
    tail = jnp.where(sublane == 0, kernel[chunks - 1 : chunks], 0.0)
    for shift in range(LANES):
        inside = lane < LANES - shift
        base = shift * 3 * chunks
        table_ref[base : base + chunks, :] = jnp.zeros((chunks, LANES), jnp.float32)
        table_ref[base + chunks : base + 2 * chunks, :] = pltpu.roll(jnp.where(inside, kernel, moved), shift, 1)
        table_ref[base + 2 * chunks : base + 3 * chunks, :] = pltpu.roll(jnp.where(inside, 0.0, tail), shift, 1)
    time_copy.wait()
    first_copy.wait()

    stride = stage_ref.shape[0] // chunks

    def shape(chunk, carry):
        def eight(eighth, carry):
            for k in range(8):
                index = eighth * 8 + k
                time = time_smem[chunk, index]
                begin = (time & (LANES - 1)) * (3 * chunks) + chunks - (time >> 7)
                stage_ref[pl.ds(index, chunks, stride=stride), :] = table_ref[pl.ds(begin, chunks), :]
            return carry

        lax.fori_loop(0, LANES // 8, eight, 0)
        at = pl.ds(pl.multiple_of(chunk * LANES, LANES), LANES)
        for c in range(chunks):
            value = stage_ref[c * stride : c * stride + LANES, :]
            high = value.astype(jnp.bfloat16)
            high_ref[c, at, :] = high
            low_ref[c, at, :] = (value - high.astype(jnp.float32)).astype(jnp.bfloat16)
        return carry

    lax.fori_loop(0, filled, shape, 0)
    beyond = pl.ds(pl.multiple_of(filled * LANES, LANES), LANES)
    for c in range(chunks):
        high_ref[c, beyond, :] = jnp.zeros((LANES, LANES), jnp.bfloat16)
        low_ref[c, beyond, :] = jnp.zeros((LANES, LANES), jnp.bfloat16)

    wide = 2 * LANES
    spot = iota((1, wide), 1)
    padded = -(-row_count // 8) * 8
    row = iota((padded, wide), 0)

    def weights(group, begin):
        chunk, offset = begin // LANES, begin % LANES
        window = jnp.concatenate([feature_ref[chunk], feature_ref[chunk + 1]], axis=1)
        window = pltpu.roll(jnp.concatenate([window, window], axis=0), wide - offset, 1)
        window = jnp.where(
            spot < WINDOW,
            window,
            jnp.where(spot < 2 * WINDOW, pltpu.roll(window, WINDOW, 1), pltpu.roll(window, 2 * WINDOW, 1)),
        )
        charge = jnp.where(spot < 3 * WINDOW, window[0:1], 0.0)
        below, column = window[1:2].astype(jnp.int32) - 1 - row, window[2:3].astype(jnp.int32)
        masks = [below == a for a in range(3)]
        blocks = []
        for k in range(GROUP):
            beside = column - (group * GROUP + k - 1)
            terms = []
            for a in range(3):
                gain = jnp.where(
                    beside == 0,
                    response_ref[a, 0],
                    jnp.where(beside == 1, response_ref[a, 1], jnp.where(beside == 2, response_ref[a, 2], 0.0)),
                )
                term = charge * gain
                high = term.astype(jnp.bfloat16).astype(jnp.float32)
                terms.append(jnp.where(spot < 2 * WINDOW, high, term - high))
            blocks.append(
                jnp.where(masks[0], terms[0], jnp.where(masks[1], terms[1], jnp.where(masks[2], terms[2], 0.0)))
            )
        return jnp.concatenate(blocks, axis=0).astype(jnp.bfloat16)

    def product(group, begin, c, held):
        at = pl.ds(pl.multiple_of(begin, 16), WINDOW)
        filler = jnp.zeros((wide - 3 * WINDOW, LANES), jnp.bfloat16)
        high = [high_ref[k, at, :] for k in (c, c + 1)]
        low = [low_ref[k, at, :] for k in (c, c + 1)]
        columns = [jnp.concatenate([h, l, h, filler], axis=0) for h, l in zip(high, low)]
        values = jnp.dot(held, jnp.concatenate(columns, axis=1), preferred_element_type=jnp.float32)
        return values.reshape(GROUP, padded, wide)[:, :row_count]

    def produce(group, carry):
        start = first_smem[2 * group, 0]
        stop = first_smem[2 * group + 3, 0]
        begin = start // 16 * 16
        pads = pl.ds(group * GROUP, GROUP)
        held = weights(group, begin)
        for c in range(0, chunks, 2):
            result_ref[pads, :, c * LANES : (c + 2) * LANES] = product(group, begin, c, held)

        def more(turn, carry):
            later = begin + turn * WINDOW
            held = weights(group, later)
            for c in range(0, chunks, 2):
                at = (pads, slice(None), slice(c * LANES, (c + 2) * LANES))
                result_ref[at] = result_ref[at] + product(group, later, c, held)
            return carry

        lax.fori_loop(1, (stop - begin + WINDOW - 1) // WINDOW, more, 0)
        pltpu.make_async_copy(result_ref.at[pads], out_ref.at[pads], out_sems.at[group]).start()
        return carry

    groups = PPR // GROUP
    lax.fori_loop(0, groups, produce, 0)

    def finish(group, carry):
        pads = pl.ds(group * GROUP, GROUP)
        pltpu.make_async_copy(result_ref.at[pads], out_ref.at[pads], out_sems.at[group]).wait()
        return carry

    lax.fori_loop(0, groups, finish, 0)


def body(charge, pad_row, pad_column, time_bin, slab_owner, block_count, shaping, response):
    slabs, pads = lax.axis_size("tm"), lax.axis_size("pad")
    rows = charge.shape[1]
    capacity = max(16, 3 * rows // (2 * slabs))
    room = LANES // 2
    assert capacity <= room and slabs % 2 == 0
    row_count = PROWS // pads
    vmem, smem = pl.BlockSpec(memory_space=pltpu.VMEM), pl.BlockSpec(memory_space=pltpu.SMEM)
    sources = (block_count, charge, pad_row, pad_column, time_bin, slab_owner.reshape(1, rows))
    sources = tuple(pltpu.with_memory_space_constraint(source, pltpu.HBM) for source in sources)
    outgoing = pl.pallas_call(
        functools.partial(route_kernel, slabs, pads, row_count, room),
        out_shape=jax.ShapeDtypeStruct((slabs * pads, 4, LANES), jnp.float32),
        in_specs=[smem] + [pl.BlockSpec(memory_space=pltpu.HBM)] * 6,
        out_specs=vmem,
        scratch_shapes=[pltpu.SemaphoreType.DMA((6,)), pltpu.SMEM(block_count.shape, block_count.dtype)]
        + [pltpu.VMEM(source.shape, source.dtype) for source in sources[1:]],
        compiler_params=pltpu.CompilerParams(vmem_limit_bytes=32 * 2**20),
        name="route",
    )(lax.axis_index("pad").astype(jnp.int32).reshape(1), *sources)
    incoming = lax.all_to_all(outgoing, ("tm", "pad"), split_axis=0, concat_axis=0, tiled=True)

    count = slabs * pads
    step = min(count, 32)
    buckets = -(-(2 * PPR // GROUP + 2) // 8) * 8
    most = -(-slabs * 2 * capacity * min(pads, 3) // LANES)
    chunks = T_DEV // LANES
    stride = LANES + 8
    signal = pl.pallas_call(
        functools.partial(signal_kernel, row_count),
        out_shape=jax.ShapeDtypeStruct((PPR, row_count, T_DEV), jnp.float32),
        in_specs=[smem, vmem, vmem],
        out_specs=pl.BlockSpec(memory_space=pl.ANY),
        scratch_shapes=[
            pltpu.VMEM((count, 16, LANES), jnp.bfloat16),
            pltpu.VMEM((count, 1, LANES), jnp.float32),
            pltpu.VMEM((count * buckets, LANES), jnp.float32),
            pltpu.VMEM((step * buckets, 2 * LANES), jnp.float32),
            pltpu.VMEM((LANES * 3 * chunks, LANES), jnp.float32),
            pltpu.VMEM((most + 2, 4, LANES), jnp.float32),
            pltpu.VMEM((most, LANES), jnp.int32),
            pltpu.VMEM((buckets, LANES), jnp.int32),
            pltpu.VMEM((chunks * stride, LANES), jnp.float32),
            pltpu.VMEM((chunks, (most + 1) * LANES, LANES), jnp.bfloat16),
            pltpu.VMEM((chunks, (most + 1) * LANES, LANES), jnp.bfloat16),
            pltpu.VMEM((PPR, row_count, T_DEV), jnp.float32),
            pltpu.SMEM((most, LANES), jnp.int32),
            pltpu.SMEM((buckets, LANES), jnp.int32),
            pltpu.SemaphoreType.DMA,
            pltpu.SemaphoreType.DMA,
            pltpu.SemaphoreType.DMA((PPR // GROUP,)),
        ],
        compiler_params=pltpu.CompilerParams(vmem_limit_bytes=56 * 2**20),
        name="signal",
    )(response, incoming, shaping.reshape(chunks, LANES))
    return signal.transpose(1, 0, 2)


def solution(mesh):
    in_specs = (
        P("pad", "tm"),
        P("pad", "tm"),
        P("pad", "tm"),
        P("pad", "tm"),
        P("pad", "tm", None),
        P("pad", "tm"),
        P(),
        P(),
    )
    out_specs = P("pad", None, "tm")
    return jax.shard_map(body, mesh=mesh, in_specs=in_specs, out_specs=out_specs, check_vma=False)
```

```python
import functools

import jax
import jax.numpy as jnp
from jax import lax
from jax.experimental import pallas as pl
from jax.experimental.pallas import tpu as pltpu
from jax.sharding import PartitionSpec as P

PROWS = 80
PPR = 66
T_DEV = 1024

LANES = 128
GROUP = 6
BATCHES = (range(0, 6), range(6, 11))
WEIGH = 11
ROWS = 128
SORT = 256
NT = (((1,), (1,)), ((), ()))


def iota(shape, dim):
    return lax.broadcasted_iota(jnp.int32, shape, dim)


def pieces(x):
    high = x.astype(jnp.bfloat16).astype(jnp.float32)
    rest = x - high
    middle = rest.astype(jnp.bfloat16).astype(jnp.float32)
    low = rest - middle
    return jnp.concatenate([high, middle, low, jnp.zeros_like(x)], axis=0).astype(jnp.bfloat16)


def joined(x):
    return (x[0:4] + x[4:8]) + x[8:12]


def running():
    source, lane = iota((LANES, 2 * LANES), 0), iota((LANES, 2 * LANES), 1)
    return jnp.where((lane >= LANES) | (source <= lane), 1.0, 0.0).astype(jnp.bfloat16)


def route_kernel(slabs, pads, row_count, room, group_ref, *refs):
    sources, (out_ref,), (sems,), targets = refs[:6], refs[6:7], refs[7:8], refs[8:]
    copies = [pltpu.make_async_copy(*pair, sems.at[k]) for k, pair in enumerate(zip(sources, targets))]
    for copy in copies:
        copy.start()
    for copy in copies:
        copy.wait()
    count_ref, charge_ref, row_ref, column_ref, bin_ref, slab_ref = targets
    rows = charge_ref.shape[1]
    blocks = rows // LANES
    group = group_ref[0]
    sums = running()
    slab_ids = iota((slabs, LANES), 0)
    lane = iota((1, LANES), 1)
    before = jnp.zeros((slabs, LANES), jnp.float32)
    slots, values = [], []
    for block in range(blocks):
        at = pl.ds(block * LANES, LANES)
        live = lane < count_ref[0, block]
        slab = jnp.where(live, slab_ref[:, at], -1)
        marks = jnp.where(slab_ids == slab, 1.0, 0.0)
        totals = jnp.dot(marks.astype(jnp.bfloat16), sums, preferred_element_type=jnp.float32)
        rank = jnp.sum(marks * (totals[:, :LANES] + before), axis=0, keepdims=True)
        before = before + totals[:, LANES:]
        slots.append(jnp.where(live, slab * room + rank.astype(jnp.int32) - 1, -1))
        values.append(
            jnp.concatenate(
                [
                    charge_ref[:, at],
                    (row_ref[:, at] + 2).astype(jnp.float32),
                    column_ref[:, at].astype(jnp.float32),
                    bin_ref[:, at].astype(jnp.float32),
                ],
                axis=0,
            )
        )
    payload = pieces(jnp.concatenate(values, axis=1))
    slot = jnp.concatenate(slots, axis=1)
    hits = jnp.where(iota((slabs * room, rows), 0) == slot, 1.0, 0.0).astype(jnp.bfloat16)
    placed = joined(lax.dot_general(payload, hits, NT, preferred_element_type=jnp.float32))
    feature, half = iota((4, LANES), 0), iota((4, LANES), 1) // room
    for slab in range(slabs):
        tile = placed[:, slab // 2 * LANES : slab // 2 * LANES + LANES]
        if slab % 2 == 0:
            other = placed[:, (slab // 2 - 1) * LANES : slab // 2 * LANES] if slab else jnp.zeros_like(tile)
            tile = jnp.where(half == 0, tile, other)
        tile = jnp.where((feature == 3) & (half != slab % 2), tile - T_DEV, tile)
        top = jnp.where(feature == 1, jnp.where(tile == row_count + 1, 1.0, 0.0), tile)
        bottom = jnp.where(feature == 1, jnp.where(tile == 2, row_count + 2.0, 0.0), tile)
        for pad in range(pads):
            apart = pad - group
            out_ref[slab * pads + pad] = jnp.where(
                apart == 0, tile, jnp.where(apart == 1, top, jnp.where(apart == -1, bottom, 0.0))
            )


def signal_kernel(
    row_count,
    response_ref,
    slots_ref,
    shaping_ref,
    out_ref,
    payload_ref,
    place_ref,
    marks_ref,
    totals_ref,
    table_ref,
    feature_ref,
    begin_ref,
    first_ref,
    stage_ref,
    high_ref,
    low_ref,
    weight_ref,
    result_ref,
    begin_smem,
    first_smem,
    copy_sems,
    out_sems,
):
    count = slots_ref.shape[0]
    step = min(count, 32)
    parts = count // step
    buckets = first_ref.shape[0]
    chunks = T_DEV // LANES

    sums = running()
    bucket_ids = iota((buckets, LANES), 0).astype(jnp.float32)

    def mark(part, earlier):
        for k in range(step):
            block = part * step + k
            slot = slots_ref[block]
            payload_ref[block] = pieces(slot)
            column = slot[2:3] + 1.0
            group = jnp.floor((column + 0.5) * (1.0 / GROUP))
            inside = jnp.where(column - group * GROUP > 1.5, 1.0, 0.0)
            bucket = jnp.where(slot[1:2] > 0.5, 2.0 * group + inside, -1.0)
            marks_ref[pl.ds(block * buckets, buckets), :] = jnp.where(bucket_ids == bucket, 1.0, 0.0)
            earlier = earlier + jnp.where((bucket >= 0.0) & (bucket < bucket_ids), 1.0, 0.0)
        return earlier

    earlier = lax.fori_loop(0, parts, mark, jnp.zeros((buckets, LANES), jnp.float32))
    first = jnp.dot(earlier.astype(jnp.bfloat16), sums, preferred_element_type=jnp.float32)[:, LANES:]
    first_ref[...] = first.astype(jnp.int32)
    first_copy = pltpu.make_async_copy(first_ref, first_smem, copy_sems.at[0])
    first_copy.start()

    def number(part, before):
        at = pl.ds(part * step * buckets, step * buckets)
        totals_ref[...] = jnp.dot(marks_ref[at, :].astype(jnp.bfloat16), sums, preferred_element_type=jnp.float32)
        for k in range(step):
            block = part * step + k
            marks = marks_ref[pl.ds(block * buckets, buckets), :]
            within = totals_ref[k * buckets : (k + 1) * buckets, :LANES]
            place_ref[block] = jnp.sum(marks * (within + before), axis=0, keepdims=True)
            before = before + totals_ref[k * buckets : (k + 1) * buckets, LANES:]
        return before

    lax.fori_loop(0, parts, number, first)
    total = jnp.max(first).astype(jnp.int32)
    filled = jnp.maximum((total + LANES - 1) // LANES, 1)

    position = iota((SORT, LANES), 0).astype(jnp.float32)

    def sort(chunk, carry):
        wanted = position + ((chunk * SORT).astype(jnp.float32) + 1.0)

        def add(part, accum):
            hits = []
            for k in range(step):
                hits.append(jnp.where(place_ref[part * step + k] == wanted, 1.0, 0.0).astype(jnp.bfloat16))
            held = [payload_ref[part * step + k] for k in range(step)]
            return accum + lax.dot_general(
                jnp.concatenate(held, axis=1),
                jnp.concatenate(hits, axis=1),
                NT,
                preferred_element_type=jnp.float32,
            )

        placed = joined(lax.fori_loop(0, parts, add, jnp.zeros((16, SORT), jnp.float32)))
        time = placed[3:4].astype(jnp.int32)
        begin = (time & (LANES - 1)) * (3 * chunks) + chunks - (time >> 7)
        for k in range(SORT // LANES):
            at = chunk * (SORT // LANES) + k
            feature_ref[at] = placed[:, k * LANES : (k + 1) * LANES]
            begin_ref[pl.ds(at, 1), :] = begin[:, k * LANES : (k + 1) * LANES]
        return carry

    lax.fori_loop(0, (filled * LANES + SORT - 1) // SORT, sort, 0)
    begin_copy = pltpu.make_async_copy(begin_ref, begin_smem, copy_sems.at[1])
    begin_copy.start()
    first_copy.wait()

    kernel = shaping_ref[...]
    lane, sublane = iota((chunks, LANES), 1), iota((chunks, LANES), 0)
    moved = jnp.concatenate([jnp.zeros((1, LANES), jnp.float32), kernel[: chunks - 1]], axis=0)
    tail = jnp.where(sublane == 0, kernel[chunks - 1 : chunks], 0.0)
    for shift in range(LANES):
        inside = lane < LANES - shift
        base = shift * 3 * chunks
        table_ref[base : base + chunks, :] = jnp.zeros((chunks, LANES), jnp.float32)
        table_ref[base + chunks : base + 2 * chunks, :] = pltpu.roll(jnp.where(inside, kernel, moved), shift, 1)
        table_ref[base + 2 * chunks : base + 3 * chunks, :] = pltpu.roll(jnp.where(inside, 0.0, tail), shift, 1)

    spot, pad = iota((1, LANES), 1), iota((8, LANES), 0)
    padded = -(-row_count // 8) * 8
    row = iota((padded, LANES), 0)

    def window_of(group, turn):
        start, stop = first_smem[2 * group, 0], first_smem[2 * group + 3, 0]
        begin = start // 16 * 16
        limit = jnp.maximum((stop + LANES - 1) // LANES, 1) * LANES
        wanted = begin + turn * LANES
        return jnp.minimum(wanted, limit - LANES), wanted, (stop - begin + LANES - 1) // LANES, limit

    def weights(group, turn):
        begin, wanted, _, _ = window_of(group, turn)
        chunk, offset = begin // LANES, begin % LANES
        window = jnp.concatenate([feature_ref[chunk], feature_ref[chunk + 1]], axis=1)
        window = pltpu.roll(jnp.concatenate([window, window], axis=0), 2 * LANES - offset, 1)[:, :LANES]
        charge = jnp.where(spot < wanted - begin, 0.0, window[0:1])
        below = window[1:2].astype(jnp.int32) - 1
        beside = window[2:3].astype(jnp.int32) - (group * GROUP - 1) - pad
        masks = [below == row + a for a in range(3)]
        highs, lows = [], []
        for a in range(3):
            gain = jnp.where(
                beside == 0,
                response_ref[a, 0],
                jnp.where(beside == 1, response_ref[a, 1], jnp.where(beside == 2, response_ref[a, 2], 0.0)),
            )
            term = charge * gain
            high = term.astype(jnp.bfloat16).astype(jnp.float32)
            highs.append(high)
            lows.append(term - high)

        def placed(terms):
            blocks = []
            for k in range(GROUP):
                block = jnp.zeros((padded, LANES), jnp.float32)
                for mask, term in zip(masks, terms):
                    block = jnp.where(mask, term[k : k + 1], block)
                blocks.append(block)
            return jnp.concatenate(blocks, axis=0).astype(jnp.bfloat16)

        return jnp.concatenate([placed(highs), placed(lows)], axis=1)

    groups = PPR // GROUP

    def weigh(part, carry):
        for k in range(WEIGH):
            group = part * WEIGH + k
            weight_ref[group] = weights(group, 0)
        return carry

    lax.fori_loop(0, groups // WEIGH, weigh, 0)
    begin_copy.wait()

    stride = stage_ref.shape[0] // chunks

    def shape(chunk, carry):
        def some(part, carry):
            for k in range(ROWS):
                index = part * ROWS + k
                begin = begin_smem[chunk, index]
                stage_ref[pl.ds(index, chunks, stride=stride), :] = table_ref[pl.ds(begin, chunks), :]
            return carry

        lax.fori_loop(0, LANES // ROWS, some, 0)
        at = pl.ds(pl.multiple_of(chunk * LANES, LANES), LANES)
        for c in range(chunks):
            value = stage_ref[c * stride : c * stride + LANES, :]
            high = value.astype(jnp.bfloat16)
            high_ref[c, at, :] = high
            low_ref[c, at, :] = (value - high.astype(jnp.float32)).astype(jnp.bfloat16)
        return carry

    def product(begin, c, held):
        at = pl.ds(pl.multiple_of(begin, 16), LANES)
        high = jnp.concatenate([high_ref[c, at, :], high_ref[c + 1, at, :]], axis=1)
        low = jnp.concatenate([low_ref[c, at, :], low_ref[c + 1, at, :]], axis=1)
        values = jnp.dot(
            jnp.concatenate([held[:, :LANES], held], axis=1),
            jnp.concatenate([low, high, high], axis=0),
            preferred_element_type=jnp.float32,
        )
        return values.reshape(GROUP, padded, 2 * LANES)[:, :row_count]

    def send(group):
        pads = pl.ds(group * GROUP, GROUP)
        return pltpu.make_async_copy(result_ref.at[pads], out_ref.at[pads], out_sems.at[group])

    def columns(group, c):
        return pl.ds(group * GROUP, GROUP), slice(None), slice(c * LANES, (c + 2) * LANES)

    def complete(group, carry):
        def more(turn, carry):
            held = weights(group, turn)
            for c in range(0, chunks, 2):
                at = columns(group, c)
                result_ref[at] = result_ref[at] + product(window_of(group, turn)[0], c, held)
            return carry

        lax.fori_loop(1, window_of(group, 0)[2], more, 0)
        send(group).start()
        return carry

    shaped = 0
    for batch in BATCHES:
        places = [window_of(group, 0) for group in batch]
        needed = places[-1][3] // LANES
        lax.fori_loop(shaped, needed, shape, 0)
        shaped = needed
        most = functools.reduce(jnp.maximum, [windows for _, _, windows, _ in places])

        def produce(group, begin):
            for c in range(0, chunks, 2):
                result_ref[columns(group, c)] = product(begin, c, weight_ref[group])

        @pl.when(most <= 1)
        def _():
            for group, (begin, _, _, _) in zip(batch, places):
                produce(group, begin)
                send(group).start()

        @pl.when(most > 1)
        def _():
            for group, (begin, _, _, _) in zip(batch, places):
                produce(group, begin)
            lax.fori_loop(batch[0], batch[-1] + 1, complete, 0)

    def finish(group, carry):
        send(group).wait()
        return carry

    lax.fori_loop(0, groups, finish, 0)


def body(charge, pad_row, pad_column, time_bin, slab_owner, block_count, shaping, response):
    slabs, pads = lax.axis_size("tm"), lax.axis_size("pad")
    rows = charge.shape[1]
    capacity = max(16, 3 * rows // (2 * slabs))
    room = LANES // 2
    assert capacity <= room and slabs % 2 == 0 and slabs * min(pads, 3) <= 256
    row_count = PROWS // pads
    vmem, smem = pl.BlockSpec(memory_space=pltpu.VMEM), pl.BlockSpec(memory_space=pltpu.SMEM)
    sources = (block_count, charge, pad_row, pad_column, time_bin, slab_owner.reshape(1, rows))
    sources = tuple(pltpu.with_memory_space_constraint(source, pltpu.HBM) for source in sources)
    outgoing = pl.pallas_call(
        functools.partial(route_kernel, slabs, pads, row_count, room),
        out_shape=jax.ShapeDtypeStruct((slabs * pads, 4, LANES), jnp.float32),
        in_specs=[smem] + [pl.BlockSpec(memory_space=pltpu.HBM)] * 6,
        out_specs=vmem,
        scratch_shapes=[pltpu.SemaphoreType.DMA((6,)), pltpu.SMEM(block_count.shape, block_count.dtype)]
        + [pltpu.VMEM(source.shape, source.dtype) for source in sources[1:]],
        compiler_params=pltpu.CompilerParams(vmem_limit_bytes=32 * 2**20),
        name="route",
    )(lax.axis_index("pad").astype(jnp.int32).reshape(1), *sources)
    incoming = lax.all_to_all(outgoing, ("tm", "pad"), split_axis=0, concat_axis=0, tiled=True)

    count = slabs * pads
    step = min(count, 32)
    buckets = -(-(2 * PPR // GROUP + 2) // 8) * 8
    most = -(-slabs * 2 * capacity * min(pads, 3) // SORT) * (SORT // LANES)
    chunks = T_DEV // LANES
    stride = LANES + 8
    signal = pl.pallas_call(
        functools.partial(signal_kernel, row_count),
        out_shape=jax.ShapeDtypeStruct((PPR, row_count, T_DEV), jnp.float32),
        in_specs=[smem, vmem, vmem],
        out_specs=pl.BlockSpec(memory_space=pl.ANY),
        scratch_shapes=[
            pltpu.VMEM((count, 16, LANES), jnp.bfloat16),
            pltpu.VMEM((count, 1, LANES), jnp.float32),
            pltpu.VMEM((count * buckets, LANES), jnp.float32),
            pltpu.VMEM((step * buckets, 2 * LANES), jnp.float32),
            pltpu.VMEM((LANES * 3 * chunks, LANES), jnp.float32),
            pltpu.VMEM((most + 1, 4, LANES), jnp.float32),
            pltpu.VMEM((most, LANES), jnp.int32),
            pltpu.VMEM((buckets, LANES), jnp.int32),
            pltpu.VMEM((chunks * stride, LANES), jnp.float32),
            pltpu.VMEM((chunks, most * LANES, LANES), jnp.bfloat16),
            pltpu.VMEM((chunks, most * LANES, LANES), jnp.bfloat16),
            pltpu.VMEM((PPR // GROUP, GROUP * -(-row_count // 8) * 8, 2 * LANES), jnp.bfloat16),
            pltpu.VMEM((PPR, row_count, T_DEV), jnp.float32),
            pltpu.SMEM((most, LANES), jnp.int32),
            pltpu.SMEM((buckets, LANES), jnp.int32),
            pltpu.SemaphoreType.DMA((2,)),
            pltpu.SemaphoreType.DMA((PPR // GROUP,)),
        ],
        compiler_params=pltpu.CompilerParams(vmem_limit_bytes=56 * 2**20),
        name="signal",
    )(response, pltpu.with_memory_space_constraint(incoming, pltpu.VMEM), pltpu.with_memory_space_constraint(shaping.reshape(chunks, LANES), pltpu.VMEM))
    return signal.transpose(1, 0, 2)


def solution(mesh):
    in_specs = (
        P("pad", "tm"),
        P("pad", "tm"),
        P("pad", "tm"),
        P("pad", "tm"),
        P("pad", "tm", None),
        P("pad", "tm"),
        P(),
        P(),
    )
    out_specs = P("pad", None, "tm")
    return jax.shard_map(body, mesh=mesh, in_specs=in_specs, out_specs=out_specs, check_vma=False)
```

```python
import functools

import jax
import jax.numpy as jnp
from jax import lax
from jax.experimental import pallas as pl
from jax.experimental.pallas import tpu as pltpu
from jax.sharding import PartitionSpec as P

PROWS = 80
PPR = 66
T_DEV = 1024

LANES = 128
GROUP = 6
BATCHES = (range(0, 6), range(6, 11))
WEIGH = 11
SORT = 256
NT = (((1,), (1,)), ((), ()))


def iota(shape, dim):
    return lax.broadcasted_iota(jnp.int32, shape, dim)


def pieces(x):
    high = x.astype(jnp.bfloat16).astype(jnp.float32)
    rest = x - high
    middle = rest.astype(jnp.bfloat16).astype(jnp.float32)
    low = rest - middle
    return jnp.concatenate([high, middle, low, jnp.zeros_like(x)], axis=0).astype(jnp.bfloat16)


def repeat(count, step, carry):
    return step(0, carry) if count == 1 else lax.fori_loop(0, count, step, carry)


def joined(x):
    return (x[0:4] + x[4:8]) + x[8:12]


def running():
    source, lane = iota((LANES, 2 * LANES), 0), iota((LANES, 2 * LANES), 1)
    return jnp.where((lane >= LANES) | (source <= lane), 1.0, 0.0).astype(jnp.bfloat16)


def route_kernel(slabs, pads, row_count, room, *refs):
    sources, out_ref, sems, targets = refs[:7], refs[7], refs[9], (*refs[10:], refs[8])
    copies = [pltpu.make_async_copy(*pair, sems.at[k]) for k, pair in enumerate(zip(sources, targets))]
    for copy in copies:
        copy.start()
    for copy in copies:
        copy.wait()
    count_ref, charge_ref, row_ref, column_ref, bin_ref, slab_ref, _ = targets
    rows = charge_ref.shape[1]
    blocks = rows // LANES
    group = lax.axis_index("pad")
    sums = running()
    slab_ids = iota((slabs, LANES), 0)
    lane = iota((1, LANES), 1)
    before = jnp.zeros((slabs, LANES), jnp.float32)
    slots, values = [], []
    for block in range(blocks):
        at = pl.ds(block * LANES, LANES)
        live = lane < count_ref[0, block]
        slab = jnp.where(live, slab_ref[:, at], -1)
        marks = jnp.where(slab_ids == slab, 1.0, 0.0)
        totals = jnp.dot(marks.astype(jnp.bfloat16), sums, preferred_element_type=jnp.float32)
        rank = jnp.sum(marks * (totals[:, :LANES] + before), axis=0, keepdims=True)
        before = before + totals[:, LANES:]
        slots.append(jnp.where(live, slab * room + rank.astype(jnp.int32) - 1, -1))
        values.append(
            jnp.concatenate(
                [
                    charge_ref[:, at],
                    (row_ref[:, at] + 2).astype(jnp.float32),
                    column_ref[:, at].astype(jnp.float32),
                    bin_ref[:, at].astype(jnp.float32),
                ],
                axis=0,
            )
        )
    payload = pieces(jnp.concatenate(values, axis=1))
    slot = jnp.concatenate(slots, axis=1)
    hits = jnp.where(iota((slabs * room, rows), 0) == slot, 1.0, 0.0).astype(jnp.bfloat16)
    placed = joined(lax.dot_general(payload, hits, NT, preferred_element_type=jnp.float32))
    feature, half = iota((4, LANES), 0), iota((4, LANES), 1) // room
    for slab in range(slabs):
        tile = placed[:, slab // 2 * LANES : slab // 2 * LANES + LANES]
        if slab % 2 == 0:
            other = placed[:, (slab // 2 - 1) * LANES : slab // 2 * LANES] if slab else jnp.zeros_like(tile)
            tile = jnp.where(half == 0, tile, other)
        tile = jnp.where((feature == 3) & (half != slab % 2), tile - T_DEV, tile)
        top = jnp.where(feature == 1, jnp.where(tile == row_count + 1, 1.0, 0.0), tile)
        bottom = jnp.where(feature == 1, jnp.where(tile == 2, row_count + 2.0, 0.0), tile)
        for pad in range(pads):
            apart = pad - group
            out_ref[slab * pads + pad] = jnp.where(
                apart == 0, tile, jnp.where(apart == 1, top, jnp.where(apart == -1, bottom, 0.0))
            )


def signal_kernel(
    row_count,
    response_hbm,
    slots_ref,
    shaping_ref,
    out_ref,
    response_ref,
    payload_ref,
    place_ref,
    marks_ref,
    totals_ref,
    table_ref,
    feature_ref,
    begin_ref,
    first_ref,
    stage_ref,
    high_ref,
    low_ref,
    weight_ref,
    result_ref,
    begin_smem,
    first_smem,
    copy_sems,
    begin_sems,
    out_sems,
):
    response_copy = pltpu.make_async_copy(response_hbm, response_ref, copy_sems.at[1])
    response_copy.start()
    count = slots_ref.shape[0]
    step = min(count, 32)
    parts = count // step
    buckets = first_ref.shape[0]
    chunks = T_DEV // LANES

    sums = running()
    bucket_ids = iota((buckets, LANES), 0).astype(jnp.float32)

    def mark(part, earlier):
        for k in range(step):
            block = part * step + k
            slot = slots_ref[block]
            payload_ref[block] = pieces(slot)
            column = slot[2:3] + 1.0
            group = jnp.floor((column + 0.5) * (1.0 / GROUP))
            inside = jnp.where(column - group * GROUP > 1.5, 1.0, 0.0)
            bucket = jnp.where(slot[1:2] > 0.5, 2.0 * group + inside, -1.0)
            marks_ref[pl.ds(block * buckets, buckets), :] = jnp.where(bucket_ids == bucket, 1.0, 0.0)
            earlier = earlier + jnp.where((bucket >= 0.0) & (bucket < bucket_ids), 1.0, 0.0)
        return earlier

    earlier = repeat(parts, mark, jnp.zeros((buckets, LANES), jnp.float32))
    first = jnp.dot(earlier.astype(jnp.bfloat16), sums, preferred_element_type=jnp.float32)[:, LANES:]
    first_ref[...] = first.astype(jnp.int32)
    first_copy = pltpu.make_async_copy(first_ref, first_smem, copy_sems.at[0])
    first_copy.start()

    kernel = shaping_ref[...]
    lane, sublane = iota((chunks, LANES), 1), iota((chunks, LANES), 0)
    moved = jnp.concatenate([jnp.zeros((1, LANES), jnp.float32), kernel[: chunks - 1]], axis=0)
    tail = jnp.where(sublane == 0, kernel[chunks - 1 : chunks], 0.0)
    for shift in range(LANES):
        inside = lane < LANES - shift
        base = shift * 3 * chunks
        table_ref[base : base + chunks, :] = jnp.zeros((chunks, LANES), jnp.float32)
        table_ref[base + chunks : base + 2 * chunks, :] = pltpu.roll(jnp.where(inside, kernel, moved), shift, 1)
        table_ref[base + 2 * chunks : base + 3 * chunks, :] = pltpu.roll(jnp.where(inside, 0.0, tail), shift, 1)

    def number(part, before):
        at = pl.ds(part * step * buckets, step * buckets)
        totals_ref[...] = jnp.dot(marks_ref[at, :].astype(jnp.bfloat16), sums, preferred_element_type=jnp.float32)
        for k in range(step):
            block = part * step + k
            marks = marks_ref[pl.ds(block * buckets, buckets), :]
            within = totals_ref[k * buckets : (k + 1) * buckets, :LANES]
            place_ref[block] = jnp.sum(marks * (within + before), axis=0, keepdims=True)
            before = before + totals_ref[k * buckets : (k + 1) * buckets, LANES:]
        return before

    repeat(parts, number, first)
    total = jnp.max(first).astype(jnp.int32)
    filled = jnp.maximum((total + LANES - 1) // LANES, 1)

    position = iota((SORT, LANES), 0).astype(jnp.float32)

    def sort(chunk, carry):
        wanted = position + ((chunk * SORT).astype(jnp.float32) + 1.0)

        def add(part, accum):
            hits = []
            for k in range(step):
                hits.append(jnp.where(place_ref[part * step + k] == wanted, 1.0, 0.0).astype(jnp.bfloat16))
            held = [payload_ref[part * step + k] for k in range(step)]
            return accum + lax.dot_general(
                jnp.concatenate(held, axis=1),
                jnp.concatenate(hits, axis=1),
                NT,
                preferred_element_type=jnp.float32,
            )

        placed = joined(repeat(parts, add, jnp.zeros((16, SORT), jnp.float32)))
        time = placed[3:4].astype(jnp.int32)
        begin = (time & (LANES - 1)) * (3 * chunks) + chunks - (time >> 7)
        for k in range(SORT // LANES):
            at = chunk * (SORT // LANES) + k
            feature_ref[at] = placed[:, k * LANES : (k + 1) * LANES]
            begin_ref[chunk, pl.ds(k, 1), :] = begin[:, k * LANES : (k + 1) * LANES]
        begins(chunk).start()
        return carry

    def begins(chunk):
        at = pl.ds(chunk, 1)
        return pltpu.make_async_copy(begin_ref.at[at], begin_smem.at[at], begin_sems.at[chunk])

    def arrive(chunk, carry):
        begins(chunk).wait()
        return carry

    lax.fori_loop(0, (filled * LANES + SORT - 1) // SORT, sort, 0)
    first_copy.wait()
    response_copy.wait()

    spot, pad = iota((1, LANES), 1), iota((8, LANES), 0)
    padded = -(-row_count // 8) * 8
    row = iota((padded, LANES), 0)

    def window_of(group, turn):
        start, stop = first_smem[2 * group, 0], first_smem[2 * group + 3, 0]
        begin = start // 16 * 16
        limit = jnp.maximum((stop + LANES - 1) // LANES, 1) * LANES
        wanted = begin + turn * LANES
        return jnp.minimum(wanted, limit - LANES), wanted, (stop - begin + LANES - 1) // LANES, limit

    def weights(group, turn):
        begin, wanted, _, _ = window_of(group, turn)
        chunk, offset = begin // LANES, begin % LANES
        window = jnp.concatenate([feature_ref[chunk], feature_ref[chunk + 1]], axis=1)
        window = pltpu.roll(jnp.concatenate([window, window], axis=0), 2 * LANES - offset, 1)[:, :LANES]
        charge = jnp.where(spot < wanted - begin, 0.0, window[0:1])
        below = window[1:2].astype(jnp.int32) - 1
        beside = window[2:3].astype(jnp.int32) - (group * GROUP - 1) - pad
        masks = [below == row + a for a in range(3)]
        highs, lows = [], []
        for a in range(3):
            gain = jnp.where(
                beside == 0,
                response_ref[a, 0],
                jnp.where(beside == 1, response_ref[a, 1], jnp.where(beside == 2, response_ref[a, 2], 0.0)),
            )
            term = charge * gain
            high = term.astype(jnp.bfloat16).astype(jnp.float32)
            highs.append(high)
            lows.append(term - high)

        def placed(terms):
            blocks = []
            for k in range(GROUP):
                block = jnp.zeros((padded, LANES), jnp.float32)
                for mask, term in zip(masks, terms):
                    block = jnp.where(mask, term[k : k + 1], block)
                blocks.append(block)
            return jnp.concatenate(blocks, axis=0).astype(jnp.bfloat16)

        return jnp.concatenate([placed(highs), placed(lows)], axis=1)

    groups = PPR // GROUP

    def weigh(part, carry):
        for k in range(WEIGH):
            group = part * WEIGH + k
            weight_ref[group] = weights(group, 0)
        return carry

    repeat(groups // WEIGH, weigh, 0)

    stride = stage_ref.shape[1] // chunks

    def shape(pair, carry):
        for half in range(SORT // LANES):
            for k in range(LANES):
                begin = begin_smem[pair, half, k]
                stage_ref[half, pl.ds(k, chunks, stride=stride), :] = table_ref[pl.ds(begin, chunks), :]
        for half in range(SORT // LANES):
            at = pl.ds(pl.multiple_of(pair * SORT + half * LANES, LANES), LANES)
            for c in range(chunks):
                value = stage_ref[half, c * stride : c * stride + LANES, :]
                high = value.astype(jnp.bfloat16)
                high_ref[c, at, :] = high
                low_ref[c, at, :] = (value - high.astype(jnp.float32)).astype(jnp.bfloat16)
        return carry

    def product(begin, c, held):
        at = pl.ds(pl.multiple_of(begin, 16), LANES)
        high = jnp.concatenate([high_ref[c, at, :], high_ref[c + 1, at, :]], axis=1)
        low = jnp.concatenate([low_ref[c, at, :], low_ref[c + 1, at, :]], axis=1)
        values = jnp.dot(
            jnp.concatenate([held[:, :LANES], held], axis=1),
            jnp.concatenate([low, high, high], axis=0),
            preferred_element_type=jnp.float32,
        )
        return values.reshape(GROUP, padded, 2 * LANES)[:, :row_count]

    def send(group):
        pads = pl.ds(group * GROUP, GROUP)
        return pltpu.make_async_copy(result_ref.at[pads], out_ref.at[pads], out_sems.at[group])

    def columns(group, c):
        return pl.ds(group * GROUP, GROUP), slice(None), slice(c * LANES, (c + 2) * LANES)

    def complete(group, carry):
        def more(turn, carry):
            held = weights(group, turn)
            for c in range(0, chunks, 2):
                at = columns(group, c)
                result_ref[at] = result_ref[at] + product(window_of(group, turn)[0], c, held)
            return carry

        lax.fori_loop(1, window_of(group, 0)[2], more, 0)
        send(group).start()
        return carry

    shaped, arrived = 0, 0
    for batch in BATCHES:
        places = [window_of(group, 0) for group in batch]
        needed = places[-1][3] // LANES
        turns = (needed * LANES + SORT - 1) // SORT
        if batch is BATCHES[-1]:
            turns = (filled * LANES + SORT - 1) // SORT
        lax.fori_loop(arrived, turns, arrive, 0)
        lax.fori_loop(shaped, turns, shape, 0)
        shaped, arrived = turns, turns
        most = functools.reduce(jnp.maximum, [windows for _, _, windows, _ in places])

        def produce(group, begin):
            for c in range(0, chunks, 2):
                result_ref[columns(group, c)] = product(begin, c, weight_ref[group])

        @pl.when(most <= 1)
        def _():
            for group, (begin, _, _, _) in zip(batch, places):
                produce(group, begin)
                send(group).start()

        @pl.when(most > 1)
        def _():
            for group, (begin, _, _, _) in zip(batch, places):
                produce(group, begin)
            lax.fori_loop(batch[0], batch[-1] + 1, complete, 0)

    def finish(group, carry):
        send(group).wait()
        return carry

    lax.fori_loop(0, groups, finish, 0)


def body(charge, pad_row, pad_column, time_bin, slab_owner, block_count, shaping, response):
    slabs, pads = lax.axis_size("tm"), lax.axis_size("pad")
    rows = charge.shape[1]
    capacity = max(16, 3 * rows // (2 * slabs))
    room = LANES // 2
    assert capacity <= room and slabs % 2 == 0 and slabs * min(pads, 3) <= 256
    row_count = PROWS // pads
    vmem = pl.BlockSpec(memory_space=pltpu.VMEM)
    chunks = T_DEV // LANES
    sources = (block_count, charge, pad_row, pad_column, time_bin, slab_owner.reshape(1, rows), shaping.reshape(chunks, LANES))
    sources = tuple(pltpu.with_memory_space_constraint(source, pltpu.HBM) for source in sources)
    outgoing, line = pl.pallas_call(
        functools.partial(route_kernel, slabs, pads, row_count, room),
        out_shape=(
            jax.ShapeDtypeStruct((slabs * pads, 4, LANES), jnp.float32),
            jax.ShapeDtypeStruct((chunks, LANES), jnp.float32),
        ),
        in_specs=[pl.BlockSpec(memory_space=pltpu.HBM)] * 7,
        out_specs=(vmem, vmem),
        scratch_shapes=[pltpu.SemaphoreType.DMA((7,)), pltpu.SMEM(block_count.shape, block_count.dtype)]
        + [pltpu.VMEM(source.shape, source.dtype) for source in sources[1:6]],
        compiler_params=pltpu.CompilerParams(vmem_limit_bytes=32 * 2**20),
        name="route",
    )(*sources)
    incoming = lax.all_to_all(outgoing, ("tm", "pad"), split_axis=0, concat_axis=0, tiled=True)

    count = slabs * pads
    step = min(count, 32)
    buckets = -(-(2 * PPR // GROUP + 2) // 8) * 8
    most = -(-slabs * 2 * capacity * min(pads, 3) // SORT) * (SORT // LANES)
    stride = LANES + 4
    signal = pl.pallas_call(
        functools.partial(signal_kernel, row_count),
        out_shape=jax.ShapeDtypeStruct((PPR, row_count, T_DEV), jnp.float32),
        in_specs=[pl.BlockSpec(memory_space=pltpu.HBM), vmem, vmem],
        out_specs=pl.BlockSpec(memory_space=pl.ANY),
        scratch_shapes=[
            pltpu.SMEM(response.shape, response.dtype),
            pltpu.VMEM((count, 16, LANES), jnp.bfloat16),
            pltpu.VMEM((count, 1, LANES), jnp.float32),
            pltpu.VMEM((count * buckets, LANES), jnp.float32),
            pltpu.VMEM((step * buckets, 2 * LANES), jnp.float32),
            pltpu.VMEM((LANES * 3 * chunks, LANES), jnp.float32),
            pltpu.VMEM((most + 1, 4, LANES), jnp.float32),
            pltpu.VMEM((most * LANES // SORT, SORT // LANES, LANES), jnp.int32),
            pltpu.VMEM((buckets, LANES), jnp.int32),
            pltpu.VMEM((SORT // LANES, chunks * stride, LANES), jnp.float32),
            pltpu.VMEM((chunks, most * LANES, LANES), jnp.bfloat16),
            pltpu.VMEM((chunks, most * LANES, LANES), jnp.bfloat16),
            pltpu.VMEM((PPR // GROUP, GROUP * -(-row_count // 8) * 8, 2 * LANES), jnp.bfloat16),
            pltpu.VMEM((PPR, row_count, T_DEV), jnp.float32),
            pltpu.SMEM((most * LANES // SORT, SORT // LANES, LANES), jnp.int32),
            pltpu.SMEM((buckets, LANES), jnp.int32),
            pltpu.SemaphoreType.DMA((2,)),
            pltpu.SemaphoreType.DMA((most * LANES // SORT,)),
            pltpu.SemaphoreType.DMA((PPR // GROUP,)),
        ],
        compiler_params=pltpu.CompilerParams(vmem_limit_bytes=56 * 2**20),
        name="signal",
    )(pltpu.with_memory_space_constraint(response, pltpu.HBM), pltpu.with_memory_space_constraint(incoming, pltpu.VMEM), pltpu.with_memory_space_constraint(line, pltpu.VMEM))
    return signal.transpose(1, 0, 2)


def solution(mesh):
    in_specs = (
        P("pad", "tm"),
        P("pad", "tm"),
        P("pad", "tm"),
        P("pad", "tm"),
        P("pad", "tm", None),
        P("pad", "tm"),
        P(),
        P(),
    )
    out_specs = P("pad", None, "tm")
    return jax.shard_map(body, mesh=mesh, in_specs=in_specs, out_specs=out_specs, check_vma=False)
```

```python
import functools

import jax
import jax.numpy as jnp
from jax import lax
from jax.experimental import pallas as pl
from jax.experimental.pallas import tpu as pltpu
from jax.sharding import PartitionSpec as P

PROWS = 80
PPR = 66
T_DEV = 1024

LANES = 128
GROUP = 6
BATCHES = (range(0, 6), range(6, 11))
WEIGH = 11
SORT = 1024
NT = (((1,), (1,)), ((), ()))


def iota(shape, dim):
    return lax.broadcasted_iota(jnp.int32, shape, dim)


def thirds(x):
    high = x.astype(jnp.bfloat16).astype(jnp.float32)
    rest = x - high
    middle = rest.astype(jnp.bfloat16).astype(jnp.float32)
    return high, middle, rest - middle


def repeat(count, step, carry):
    return step(0, carry) if count == 1 else lax.fori_loop(0, count, step, carry)


def joined(x):
    return (x[0:4] + x[4:8]) + x[8:12]


def running():
    source, lane = iota((LANES, 2 * LANES), 0), iota((LANES, 2 * LANES), 1)
    return jnp.where((lane >= LANES) | (source <= lane), 1.0, 0.0).astype(jnp.bfloat16)


def route_kernel(slabs, pads, row_count, room, *refs):
    sources, out_ref, sems, targets = refs[:7], refs[7], refs[9], (*refs[10:], refs[8])
    copies = [pltpu.make_async_copy(*pair, sems.at[k]) for k, pair in enumerate(zip(sources, targets))]
    for copy in copies:
        copy.start()
    for copy in copies:
        copy.wait()
    count_ref, charge_ref, row_ref, column_ref, bin_ref, slab_ref, _ = targets
    rows = charge_ref.shape[1]
    blocks = rows // LANES
    group = lax.axis_index("pad")
    sums = running()
    slab_ids, row_slabs = iota((slabs, LANES), 0), iota((4 * slabs, LANES), 0) // 4
    lane = iota((1, LANES), 1)
    wanted = (iota((LANES, LANES), 0) % room + 1).astype(jnp.float32)
    before = jnp.zeros((slabs, LANES), jnp.float32)
    rows_of, hits = [], []
    for block in range(blocks):
        at = pl.ds(block * LANES, LANES)
        live = lane < count_ref[0, block]
        slab = jnp.where(live, slab_ref[:, at], -1)
        marks = jnp.where(slab_ids == slab, 1.0, 0.0)
        totals = jnp.dot(marks.astype(jnp.bfloat16), sums, preferred_element_type=jnp.float32)
        rank = jnp.sum(marks * (totals[:, :LANES] + before), axis=0, keepdims=True)
        before = before + totals[:, LANES:]
        hits.append(jnp.where(wanted == rank, 1.0, 0.0).astype(jnp.bfloat16))
        value = jnp.concatenate(
            [
                charge_ref[:, at],
                (row_ref[:, at] + 2).astype(jnp.float32),
                column_ref[:, at].astype(jnp.float32),
                bin_ref[:, at].astype(jnp.float32),
            ],
            axis=0,
        )
        here = row_slabs == slab
        terms = []
        for term in thirds(jnp.concatenate([value, value], axis=0)):
            terms.append(jnp.where(here, jnp.concatenate([term] * (slabs // 2), axis=0), 0.0))
        rows_of.append(jnp.concatenate(terms, axis=0).astype(jnp.bfloat16))
    sent = lax.dot_general(
        jnp.concatenate(rows_of, axis=1), jnp.concatenate(hits, axis=1), NT, preferred_element_type=jnp.float32
    )
    sent = (sent[: 4 * slabs] + sent[4 * slabs : 8 * slabs]) + sent[8 * slabs :]
    earlier = jnp.concatenate([jnp.zeros((4, LANES), jnp.float32), sent[:-4]], axis=0)
    feature, late = iota((4 * slabs, LANES), 0) % 4, iota((4 * slabs, LANES), 1) >= room
    sent = jnp.where(late, earlier, sent)
    sent = jnp.where((feature == 3) & late, sent - T_DEV, sent)
    top = jnp.where(feature == 1, jnp.where(sent == row_count + 1, 1.0, 0.0), sent)
    bottom = jnp.where(feature == 1, jnp.where(sent == 2, row_count + 2.0, 0.0), sent)
    for pad in range(pads):
        apart = pad - group
        chosen = jnp.where(apart == 0, sent, jnp.where(apart == 1, top, jnp.where(apart == -1, bottom, 0.0)))
        for slab in range(slabs):
            out_ref[slab * pads + pad] = chosen[4 * slab : 4 * slab + 4]


def signal_kernel(
    row_count,
    response_hbm,
    slots_ref,
    shaping_ref,
    out_ref,
    response_ref,
    payload_ref,
    place_ref,
    marks_ref,
    totals_ref,
    table_ref,
    feature_ref,
    begin_ref,
    first_ref,
    stage_ref,
    high_ref,
    low_ref,
    weight_ref,
    result_ref,
    begin_smem,
    first_smem,
    copy_sems,
    begin_sems,
    out_sems,
):
    response_copy = pltpu.make_async_copy(response_hbm, response_ref, copy_sems.at[1])
    response_copy.start()
    count = slots_ref.shape[0]
    step = min(count, 32)
    parts = count // step
    buckets = first_ref.shape[0]
    chunks = T_DEV // LANES

    sums = running()
    bucket_ids = iota((buckets, LANES), 0).astype(jnp.float32)

    def mark(part, earlier):
        for k in range(step):
            block = part * step + k
            slot = slots_ref[block]
            payload_ref[block] = jnp.concatenate([*thirds(slot), jnp.zeros_like(slot)], axis=0)
            column = slot[2:3] + 1.0
            group = jnp.floor((column + 0.5) * (1.0 / GROUP))
            inside = jnp.where(column - group * GROUP > 1.5, 1.0, 0.0)
            bucket = jnp.where(slot[1:2] > 0.5, 2.0 * group + inside, -1.0)
            marks_ref[pl.ds(block * buckets, buckets), :] = jnp.where(bucket_ids == bucket, 1.0, 0.0)
            earlier = earlier + jnp.where((bucket >= 0.0) & (bucket < bucket_ids), 1.0, 0.0)
        return earlier

    earlier = repeat(parts, mark, jnp.zeros((buckets, LANES), jnp.float32))
    first = jnp.dot(earlier.astype(jnp.bfloat16), sums, preferred_element_type=jnp.float32)[:, LANES:]
    first_ref[...] = first.astype(jnp.int32)
    first_copy = pltpu.make_async_copy(first_ref, first_smem, copy_sems.at[0])
    first_copy.start()

    kernel = shaping_ref[...]
    lane, sublane = iota((chunks, LANES), 1), iota((chunks, LANES), 0)
    moved = jnp.concatenate([jnp.zeros((1, LANES), jnp.float32), kernel[: chunks - 1]], axis=0)
    tail = jnp.where(sublane == 0, kernel[chunks - 1 : chunks], 0.0)
    for shift in range(LANES):
        inside = lane < LANES - shift
        base = shift * 3 * chunks
        table_ref[base : base + chunks, :] = jnp.zeros((chunks, LANES), jnp.float32)
        table_ref[base + chunks : base + 2 * chunks, :] = pltpu.roll(jnp.where(inside, kernel, moved), shift, 1)
        table_ref[base + 2 * chunks : base + 3 * chunks, :] = pltpu.roll(jnp.where(inside, 0.0, tail), shift, 1)

    def number(part, before):
        at = pl.ds(part * step * buckets, step * buckets)
        totals_ref[...] = jnp.dot(marks_ref[at, :].astype(jnp.bfloat16), sums, preferred_element_type=jnp.float32)
        for k in range(step):
            block = part * step + k
            marks = marks_ref[pl.ds(block * buckets, buckets), :]
            within = totals_ref[k * buckets : (k + 1) * buckets, :LANES]
            place_ref[block] = jnp.sum(marks * (within + before), axis=0, keepdims=True)
            before = before + totals_ref[k * buckets : (k + 1) * buckets, LANES:]
        return before

    repeat(parts, number, first)
    total = jnp.max(first).astype(jnp.int32)
    filled = jnp.maximum((total + LANES - 1) // LANES, 1)

    position = iota((LANES, LANES), 0).astype(jnp.float32)

    def sort(turn, carry):
        base = (turn * SORT).astype(jnp.float32) + 1.0

        def add(part, accum):
            hits, held = [], []
            for k in range(step):
                place = place_ref[part * step + k] - base
                chunk = jnp.floor(place * (1.0 / LANES))
                hits.append(jnp.where(place - chunk * LANES == position, 1.0, 0.0).astype(jnp.bfloat16))
                payload = payload_ref[part * step + k]
                rows = [jnp.where(chunk == c, payload, 0.0) for c in range(SORT // LANES)]
                held.append(jnp.concatenate(rows, axis=0).astype(jnp.bfloat16))
            return accum + lax.dot_general(
                jnp.concatenate(held, axis=1),
                jnp.concatenate(hits, axis=1),
                NT,
                preferred_element_type=jnp.float32,
            )

        placed = repeat(parts, add, jnp.zeros((16 * SORT // LANES, LANES), jnp.float32))
        for k in range(SORT // LANES):
            features = joined(placed[16 * k : 16 * k + 16])
            feature_ref[turn * (SORT // LANES) + k] = features
            time = features[3:4].astype(jnp.int32)
            begin_ref[turn, pl.ds(k, 1), :] = (time & (LANES - 1)) * (3 * chunks) + chunks - (time >> 7)
        begins(turn).start()
        return carry

    def begins(turn):
        at = pl.ds(turn, 1)
        return pltpu.make_async_copy(begin_ref.at[at], begin_smem.at[at], begin_sems.at[turn])

    def arrive(turn, carry):
        begins(turn).wait()
        return carry

    turns = (filled * LANES + SORT - 1) // SORT
    lax.fori_loop(0, turns, sort, 0)
    first_copy.wait()
    response_copy.wait()

    spot, pad = iota((1, LANES), 1), iota((8, LANES), 0)
    padded = -(-row_count // 8) * 8
    row = iota((padded, LANES), 0)

    def window_of(group, turn):
        start, stop = first_smem[2 * group, 0], first_smem[2 * group + 3, 0]
        begin = start // 16 * 16
        limit = jnp.maximum((stop + LANES - 1) // LANES, 1) * LANES
        wanted = begin + turn * LANES
        return jnp.minimum(wanted, limit - LANES), wanted, (stop - begin + LANES - 1) // LANES, limit

    def weights(group, turn):
        begin, wanted, _, _ = window_of(group, turn)
        chunk, offset = begin // LANES, begin % LANES
        window = jnp.concatenate([feature_ref[chunk], feature_ref[chunk + 1]], axis=1)
        window = pltpu.roll(jnp.concatenate([window, window], axis=0), 2 * LANES - offset, 1)[:, :LANES]
        charge = jnp.where(spot < wanted - begin, 0.0, window[0:1])
        below = window[1:2].astype(jnp.int32) - 1
        beside = window[2:3].astype(jnp.int32) - (group * GROUP - 1) - pad
        masks = [below == row + a for a in range(3)]
        highs, lows = [], []
        for a in range(3):
            gain = jnp.where(
                beside == 0,
                response_ref[a, 0],
                jnp.where(beside == 1, response_ref[a, 1], jnp.where(beside == 2, response_ref[a, 2], 0.0)),
            )
            term = charge * gain
            high = term.astype(jnp.bfloat16).astype(jnp.float32)
            highs.append(high)
            lows.append(term - high)

        def placed(terms):
            blocks = []
            for k in range(GROUP):
                block = jnp.zeros((padded, LANES), jnp.float32)
                for mask, term in zip(masks, terms):
                    block = jnp.where(mask, term[k : k + 1], block)
                blocks.append(block)
            return jnp.concatenate(blocks, axis=0).astype(jnp.bfloat16)

        return jnp.concatenate([placed(highs), placed(lows)], axis=1)

    groups = PPR // GROUP

    def weigh(part, carry):
        for k in range(WEIGH):
            group = part * WEIGH + k
            weight_ref[group] = weights(group, 0)
        return carry

    repeat(groups // WEIGH, weigh, 0)

    lax.fori_loop(0, turns, arrive, 0)

    stride = stage_ref.shape[1] // chunks

    def shape(pair, carry):
        for half in range(2):
            chunk = pair * 2 + half
            for k in range(LANES):
                begin = begin_smem[chunk // (SORT // LANES), chunk % (SORT // LANES), k]
                stage_ref[half, pl.ds(k, chunks, stride=stride), :] = table_ref[pl.ds(begin, chunks), :]
        for half in range(2):
            at = pl.ds(pl.multiple_of((pair * 2 + half) * LANES, LANES), LANES)
            for c in range(chunks):
                value = stage_ref[half, c * stride : c * stride + LANES, :]
                high = value.astype(jnp.bfloat16)
                high_ref[c, at, :] = high
                low_ref[c, at, :] = (value - high.astype(jnp.float32)).astype(jnp.bfloat16)
        return carry

    def product(begin, c, held):
        at = pl.ds(pl.multiple_of(begin, 16), LANES)
        high = jnp.concatenate([high_ref[c, at, :], high_ref[c + 1, at, :]], axis=1)
        low = jnp.concatenate([low_ref[c, at, :], low_ref[c + 1, at, :]], axis=1)
        values = jnp.dot(
            jnp.concatenate([held[:, :LANES], held], axis=1),
            jnp.concatenate([low, high, high], axis=0),
            preferred_element_type=jnp.float32,
        )
        return values.reshape(GROUP, padded, 2 * LANES)[:, :row_count]

    def send(group):
        pads = pl.ds(group * GROUP, GROUP)
        return pltpu.make_async_copy(result_ref.at[pads], out_ref.at[pads], out_sems.at[group])

    def columns(group, c):
        return pl.ds(group * GROUP, GROUP), slice(None), slice(c * LANES, (c + 2) * LANES)

    def complete(group, carry):
        def more(turn, carry):
            held = weights(group, turn)
            for c in range(0, chunks, 2):
                at = columns(group, c)
                result_ref[at] = result_ref[at] + product(window_of(group, turn)[0], c, held)
            return carry

        lax.fori_loop(1, window_of(group, 0)[2], more, 0)
        send(group).start()
        return carry

    shaped = 0
    for batch in BATCHES:
        places = [window_of(group, 0) for group in batch]
        needed = places[-1][3] // LANES
        lax.fori_loop(shaped, (needed + 1) // 2, shape, 0)
        shaped = (needed + 1) // 2
        most = functools.reduce(jnp.maximum, [windows for _, _, windows, _ in places])

        def produce(group, begin):
            for c in range(0, chunks, 2):
                result_ref[columns(group, c)] = product(begin, c, weight_ref[group])

        @pl.when(most <= 1)
        def _():
            for group, (begin, _, _, _) in zip(batch, places):
                produce(group, begin)
                send(group).start()

        @pl.when(most > 1)
        def _():
            for group, (begin, _, _, _) in zip(batch, places):
                produce(group, begin)
            lax.fori_loop(batch[0], batch[-1] + 1, complete, 0)

    def finish(group, carry):
        send(group).wait()
        return carry

    lax.fori_loop(0, groups, finish, 0)


def body(charge, pad_row, pad_column, time_bin, slab_owner, block_count, shaping, response):
    slabs, pads = lax.axis_size("tm"), lax.axis_size("pad")
    rows = charge.shape[1]
    capacity = max(16, 3 * rows // (2 * slabs))
    room = LANES // 2
    assert capacity <= room and slabs % 2 == 0 and slabs * min(pads, 3) <= 256
    row_count = PROWS // pads
    vmem = pl.BlockSpec(memory_space=pltpu.VMEM)
    chunks = T_DEV // LANES
    sources = (block_count, charge, pad_row, pad_column, time_bin, slab_owner.reshape(1, rows), shaping.reshape(chunks, LANES))
    sources = tuple(pltpu.with_memory_space_constraint(source, pltpu.HBM) for source in sources)
    outgoing, line = pl.pallas_call(
        functools.partial(route_kernel, slabs, pads, row_count, room),
        out_shape=(
            jax.ShapeDtypeStruct((slabs * pads, 4, LANES), jnp.float32),
            jax.ShapeDtypeStruct((chunks, LANES), jnp.float32),
        ),
        in_specs=[pl.BlockSpec(memory_space=pltpu.HBM)] * 7,
        out_specs=(vmem, vmem),
        scratch_shapes=[pltpu.SemaphoreType.DMA((7,)), pltpu.SMEM(block_count.shape, block_count.dtype)]
        + [pltpu.VMEM(source.shape, source.dtype) for source in sources[1:6]],
        compiler_params=pltpu.CompilerParams(vmem_limit_bytes=32 * 2**20),
        name="route",
    )(*sources)
    incoming = lax.all_to_all(outgoing, ("tm", "pad"), split_axis=0, concat_axis=0, tiled=True)

    count = slabs * pads
    step = min(count, 32)
    buckets = -(-(2 * PPR // GROUP + 2) // 8) * 8
    most = -(-slabs * 2 * capacity * min(pads, 3) // SORT) * (SORT // LANES)
    stride = LANES + 4
    signal = pl.pallas_call(
        functools.partial(signal_kernel, row_count),
        out_shape=jax.ShapeDtypeStruct((PPR, row_count, T_DEV), jnp.float32),
        in_specs=[pl.BlockSpec(memory_space=pltpu.HBM), vmem, vmem],
        out_specs=pl.BlockSpec(memory_space=pl.ANY),
        scratch_shapes=[
            pltpu.SMEM(response.shape, response.dtype),
            pltpu.VMEM((count, 16, LANES), jnp.float32),
            pltpu.VMEM((count, 1, LANES), jnp.float32),
            pltpu.VMEM((count * buckets, LANES), jnp.float32),
            pltpu.VMEM((step * buckets, 2 * LANES), jnp.float32),
            pltpu.VMEM((LANES * 3 * chunks, LANES), jnp.float32),
            pltpu.VMEM((most + 1, 4, LANES), jnp.float32),
            pltpu.VMEM((most * LANES // SORT, SORT // LANES, LANES), jnp.int32),
            pltpu.VMEM((buckets, LANES), jnp.int32),
            pltpu.VMEM((2, chunks * stride, LANES), jnp.float32),
            pltpu.VMEM((chunks, most * LANES, LANES), jnp.bfloat16),
            pltpu.VMEM((chunks, most * LANES, LANES), jnp.bfloat16),
            pltpu.VMEM((PPR // GROUP, GROUP * -(-row_count // 8) * 8, 2 * LANES), jnp.bfloat16),
            pltpu.VMEM((PPR, row_count, T_DEV), jnp.float32),
            pltpu.SMEM((most * LANES // SORT, SORT // LANES, LANES), jnp.int32),
            pltpu.SMEM((buckets, LANES), jnp.int32),
            pltpu.SemaphoreType.DMA((2,)),
            pltpu.SemaphoreType.DMA((most * LANES // SORT,)),
            pltpu.SemaphoreType.DMA((PPR // GROUP,)),
        ],
        compiler_params=pltpu.CompilerParams(vmem_limit_bytes=56 * 2**20),
        name="signal",
    )(pltpu.with_memory_space_constraint(response, pltpu.HBM), pltpu.with_memory_space_constraint(incoming, pltpu.VMEM), pltpu.with_memory_space_constraint(line, pltpu.VMEM))
    return signal.transpose(1, 0, 2)


def solution(mesh):
    in_specs = (
        P("pad", "tm"),
        P("pad", "tm"),
        P("pad", "tm"),
        P("pad", "tm"),
        P("pad", "tm", None),
        P("pad", "tm"),
        P(),
        P(),
    )
    out_specs = P("pad", None, "tm")
    return jax.shard_map(body, mesh=mesh, in_specs=in_specs, out_specs=out_specs, check_vma=False)
```

```python
import functools

import jax
import jax.numpy as jnp
from jax import lax
from jax.experimental import pallas as pl
from jax.experimental.pallas import tpu as pltpu
from jax.sharding import PartitionSpec as P

PROWS = 80
PPR = 66
T_DEV = 1024

LANES = 128
GROUP = 6
BATCHES = (range(0, 6), range(6, 11))
SORT = 1024
NT = (((1,), (1,)), ((), ()))


def iota(shape, dim):
    return lax.broadcasted_iota(jnp.int32, shape, dim)


def thirds(x):
    high = x.astype(jnp.bfloat16).astype(jnp.float32)
    rest = x - high
    middle = rest.astype(jnp.bfloat16).astype(jnp.float32)
    return high, middle, rest - middle


def repeat(count, step, carry):
    return step(0, carry) if count == 1 else lax.fori_loop(0, count, step, carry)


def joined(x):
    return (x[0:4] + x[4:8]) + x[8:12]


def running():
    source, lane = iota((LANES, 2 * LANES), 0), iota((LANES, 2 * LANES), 1)
    return jnp.where((lane >= LANES) | (source <= lane), 1.0, 0.0).astype(jnp.bfloat16)


def route_kernel(slabs, pads, row_count, room, *refs):
    sources, out_ref, sems, targets = refs[:7], refs[7], refs[9], (*refs[10:], refs[8])
    copies = [pltpu.make_async_copy(*pair, sems.at[k]) for k, pair in enumerate(zip(sources, targets))]
    for copy in copies:
        copy.start()
    for copy in copies:
        copy.wait()
    count_ref, charge_ref, row_ref, column_ref, bin_ref, slab_ref, _ = targets
    rows = charge_ref.shape[1]
    blocks = rows // LANES
    group = lax.axis_index("pad")
    sums = running()
    slab_ids, row_slabs = iota((slabs, LANES), 0), iota((4 * slabs, LANES), 0) // 4
    lane = iota((1, LANES), 1)
    wanted = (iota((LANES, LANES), 0) % room + 1).astype(jnp.float32)
    before = jnp.zeros((slabs, LANES), jnp.float32)
    rows_of, hits = [], []
    for block in range(blocks):
        at = pl.ds(block * LANES, LANES)
        live = lane < count_ref[0, block]
        slab = jnp.where(live, slab_ref[:, at], -1)
        marks = jnp.where(slab_ids == slab, 1.0, 0.0)
        totals = jnp.dot(marks.astype(jnp.bfloat16), sums, preferred_element_type=jnp.float32)
        rank = jnp.sum(marks * (totals[:, :LANES] + before), axis=0, keepdims=True)
        before = before + totals[:, LANES:]
        hits.append(jnp.where(wanted == rank, 1.0, 0.0).astype(jnp.bfloat16))
        value = jnp.concatenate(
            [
                charge_ref[:, at],
                (row_ref[:, at] + 2).astype(jnp.float32),
                column_ref[:, at].astype(jnp.float32),
                bin_ref[:, at].astype(jnp.float32),
            ],
            axis=0,
        )
        here = row_slabs == slab
        terms = []
        for term in thirds(jnp.concatenate([value, value], axis=0)):
            terms.append(jnp.where(here, jnp.concatenate([term] * (slabs // 2), axis=0), 0.0))
        rows_of.append(jnp.concatenate(terms, axis=0).astype(jnp.bfloat16))
    sent = lax.dot_general(
        jnp.concatenate(rows_of, axis=1), jnp.concatenate(hits, axis=1), NT, preferred_element_type=jnp.float32
    )
    sent = (sent[: 4 * slabs] + sent[4 * slabs : 8 * slabs]) + sent[8 * slabs :]
    earlier = jnp.concatenate([jnp.zeros((4, LANES), jnp.float32), sent[:-4]], axis=0)
    feature, late = iota((4 * slabs, LANES), 0) % 4, iota((4 * slabs, LANES), 1) >= room
    sent = jnp.where(late, earlier, sent)
    sent = jnp.where((feature == 3) & late, sent - T_DEV, sent)
    top = jnp.where(feature == 1, jnp.where(sent == row_count + 1, 1.0, 0.0), sent)
    bottom = jnp.where(feature == 1, jnp.where(sent == 2, row_count + 2.0, 0.0), sent)
    for pad in range(pads):
        apart = pad - group
        chosen = jnp.where(apart == 0, sent, jnp.where(apart == 1, top, jnp.where(apart == -1, bottom, 0.0)))
        for slab in range(slabs):
            out_ref[slab * pads + pad] = chosen[4 * slab : 4 * slab + 4]


def signal_kernel(
    row_count,
    response_hbm,
    slots_ref,
    shaping_ref,
    out_ref,
    response_ref,
    payload_ref,
    place_ref,
    marks_ref,
    totals_ref,
    table_ref,
    feature_ref,
    begin_ref,
    first_ref,
    stage_ref,
    high_ref,
    low_ref,
    weight_ref,
    result_ref,
    begin_smem,
    first_smem,
    copy_sems,
    begin_sems,
    out_sems,
):
    response_copy = pltpu.make_async_copy(response_hbm, response_ref, copy_sems.at[1])
    response_copy.start()
    count = slots_ref.shape[0]
    step = min(count, 32)
    parts = count // step
    buckets = first_ref.shape[0]
    chunks = T_DEV // LANES

    sums = running()
    bucket_ids = iota((buckets, LANES), 0).astype(jnp.float32)

    def mark(part, earlier):
        for k in range(step):
            block = part * step + k
            slot = slots_ref[block]
            payload_ref[block] = jnp.concatenate([*thirds(slot), jnp.zeros_like(slot)], axis=0)
            column = slot[2:3] + 1.0
            group = jnp.floor((column + 0.5) * (1.0 / GROUP))
            inside = jnp.where(column - group * GROUP > 1.5, 1.0, 0.0)
            bucket = jnp.where(slot[1:2] > 0.5, 2.0 * group + inside, -1.0)
            marks_ref[pl.ds(block * buckets, buckets), :] = jnp.where(bucket_ids == bucket, 1.0, 0.0)
            earlier = earlier + jnp.where((bucket >= 0.0) & (bucket < bucket_ids), 1.0, 0.0)
        return earlier

    earlier = repeat(parts, mark, jnp.zeros((buckets, LANES), jnp.float32))
    first = jnp.dot(earlier.astype(jnp.bfloat16), sums, preferred_element_type=jnp.float32)[:, LANES:]
    first_ref[...] = first.astype(jnp.int32)
    first_copy = pltpu.make_async_copy(first_ref, first_smem, copy_sems.at[0])
    first_copy.start()

    def number(part, before):
        at = pl.ds(part * step * buckets, step * buckets)
        totals_ref[...] = jnp.dot(marks_ref[at, :].astype(jnp.bfloat16), sums, preferred_element_type=jnp.float32)
        for k in range(step):
            block = part * step + k
            marks = marks_ref[pl.ds(block * buckets, buckets), :]
            within = totals_ref[k * buckets : (k + 1) * buckets, :LANES]
            place_ref[block] = jnp.sum(marks * (within + before), axis=0, keepdims=True)
            before = before + totals_ref[k * buckets : (k + 1) * buckets, LANES:]
        return before

    repeat(parts, number, first)
    total = jnp.max(first).astype(jnp.int32)
    filled = jnp.maximum((total + LANES - 1) // LANES, 1)

    position = iota((LANES, LANES), 0).astype(jnp.float32)

    def sort(turn, carry):
        base = (turn * SORT).astype(jnp.float32) + 1.0

        def add(part, accum):
            hits, held = [], []
            for k in range(step):
                place = place_ref[part * step + k] - base
                chunk = jnp.floor(place * (1.0 / LANES))
                hits.append(jnp.where(place - chunk * LANES == position, 1.0, 0.0).astype(jnp.bfloat16))
                payload = payload_ref[part * step + k]
                rows = [jnp.where(chunk == c, payload, 0.0) for c in range(SORT // LANES)]
                held.append(jnp.concatenate(rows, axis=0).astype(jnp.bfloat16))
            return accum + lax.dot_general(
                jnp.concatenate(held, axis=1),
                jnp.concatenate(hits, axis=1),
                NT,
                preferred_element_type=jnp.float32,
            )

        placed = repeat(parts, add, jnp.zeros((16 * SORT // LANES, LANES), jnp.float32))
        for k in range(SORT // LANES):
            features = joined(placed[16 * k : 16 * k + 16])
            feature_ref[turn * (SORT // LANES) + k] = features
            time = features[3:4].astype(jnp.int32)
            begin_ref[turn, pl.ds(k, 1), :] = (time & (LANES - 1)) * (3 * chunks) + chunks - (time >> 7)
        begins(turn).start()
        return carry

    def begins(turn):
        at = pl.ds(turn, 1)
        return pltpu.make_async_copy(begin_ref.at[at], begin_smem.at[at], begin_sems.at[turn])

    def arrive(turn, carry):
        begins(turn).wait()
        return carry

    turns = (filled * LANES + SORT - 1) // SORT
    lax.fori_loop(0, turns, sort, 0)
    first_copy.wait()
    response_copy.wait()

    kernel = shaping_ref[...]
    lane, sublane = iota((chunks, LANES), 1), iota((chunks, LANES), 0)
    moved = jnp.concatenate([jnp.zeros((1, LANES), jnp.float32), kernel[: chunks - 1]], axis=0)
    tail = jnp.where(sublane == 0, kernel[chunks - 1 : chunks], 0.0)
    for shift in range(LANES):
        inside = lane < LANES - shift
        base = shift * 3 * chunks
        table_ref[base : base + chunks, :] = jnp.zeros((chunks, LANES), jnp.float32)
        table_ref[base + chunks : base + 2 * chunks, :] = pltpu.roll(jnp.where(inside, kernel, moved), shift, 1)
        table_ref[base + 2 * chunks : base + 3 * chunks, :] = pltpu.roll(jnp.where(inside, 0.0, tail), shift, 1)

    spot, pad = iota((1, LANES), 1), iota((8, LANES), 0)
    padded = -(-row_count // 8) * 8
    row = iota((padded, LANES), 0)

    def window_of(group, turn):
        start, stop = first_smem[2 * group, 0], first_smem[2 * group + 3, 0]
        begin = start // 16 * 16
        limit = jnp.maximum((stop + LANES - 1) // LANES, 1) * LANES
        wanted = begin + turn * LANES
        return jnp.minimum(wanted, limit - LANES), wanted, (stop - begin + LANES - 1) // LANES, limit

    def weights(group, turn):
        begin, wanted, _, _ = window_of(group, turn)
        chunk, offset = begin // LANES, begin % LANES
        window = jnp.concatenate([feature_ref[chunk], feature_ref[chunk + 1]], axis=1)
        window = pltpu.roll(jnp.concatenate([window, window], axis=0), 2 * LANES - offset, 1)[:, :LANES]
        charge = jnp.where(spot < wanted - begin, 0.0, window[0:1])
        below = window[1:2].astype(jnp.int32) - 1
        beside = window[2:3].astype(jnp.int32) - (group * GROUP - 1) - pad
        masks = [below == row + a for a in range(3)]
        highs, lows = [], []
        for a in range(3):
            gain = jnp.where(
                beside == 0,
                response_ref[a, 0],
                jnp.where(beside == 1, response_ref[a, 1], jnp.where(beside == 2, response_ref[a, 2], 0.0)),
            )
            term = charge * gain
            high = term.astype(jnp.bfloat16).astype(jnp.float32)
            highs.append(high)
            lows.append(term - high)

        def placed(terms):
            blocks = []
            for k in range(GROUP):
                block = jnp.zeros((padded, LANES), jnp.float32)
                for mask, term in zip(masks, terms):
                    block = jnp.where(mask, term[k : k + 1], block)
                blocks.append(block)
            return jnp.concatenate(blocks, axis=0).astype(jnp.bfloat16)

        return jnp.concatenate([placed(highs), placed(lows)], axis=1)

    groups = PPR // GROUP


    lax.fori_loop(0, turns, arrive, 0)

    stride = stage_ref.shape[1] // chunks

    def shape(pair, carry):
        for half in range(2):
            chunk = pair * 2 + half
            for k in range(LANES):
                begin = begin_smem[chunk // (SORT // LANES), chunk % (SORT // LANES), k]
                stage_ref[half, pl.ds(k, chunks, stride=stride), :] = table_ref[pl.ds(begin, chunks), :]
        for half in range(2):
            at = pl.ds(pl.multiple_of((pair * 2 + half) * LANES, LANES), LANES)
            for c in range(chunks):
                value = stage_ref[half, c * stride : c * stride + LANES, :]
                high = value.astype(jnp.bfloat16)
                high_ref[c, at, :] = high
                low_ref[c, at, :] = (value - high.astype(jnp.float32)).astype(jnp.bfloat16)
        return carry

    def product(begin, c, held):
        at = pl.ds(pl.multiple_of(begin, 16), LANES)
        high = jnp.concatenate([high_ref[c, at, :], high_ref[c + 1, at, :]], axis=1)
        low = jnp.concatenate([low_ref[c, at, :], low_ref[c + 1, at, :]], axis=1)
        values = jnp.dot(
            jnp.concatenate([held[:, :LANES], held], axis=1),
            jnp.concatenate([low, high, high], axis=0),
            preferred_element_type=jnp.float32,
        )
        return values.reshape(GROUP, padded, 2 * LANES)[:, :row_count]

    def send(group):
        pads = pl.ds(group * GROUP, GROUP)
        return pltpu.make_async_copy(result_ref.at[pads], out_ref.at[pads], out_sems.at[group])

    def columns(group, c):
        return pl.ds(group * GROUP, GROUP), slice(None), slice(c * LANES, (c + 2) * LANES)

    def complete(group, carry):
        def more(turn, carry):
            held = weights(group, turn)
            for c in range(0, chunks, 2):
                at = columns(group, c)
                result_ref[at] = result_ref[at] + product(window_of(group, turn)[0], c, held)
            return carry

        lax.fori_loop(1, window_of(group, 0)[2], more, 0)
        send(group).start()
        return carry

    shaped = 0
    for batch in BATCHES:
        places = [window_of(group, 0) for group in batch]
        needed = places[-1][3] // LANES
        lax.fori_loop(shaped, (needed + 1) // 2, shape, 0)
        shaped = (needed + 1) // 2
        most = functools.reduce(jnp.maximum, [windows for _, _, windows, _ in places])

        def produce(group, begin):
            for c in range(0, chunks, 2):
                result_ref[columns(group, c)] = product(begin, c, weight_ref[group])

        @pl.when(most <= 1)
        def _():
            for group in batch:
                weight_ref[group] = weights(group, 0)
            for group, (begin, _, _, _) in zip(batch, places):
                produce(group, begin)
                send(group).start()

        @pl.when(most > 1)
        def _():
            for group in batch:
                weight_ref[group] = weights(group, 0)
            for group, (begin, _, _, _) in zip(batch, places):
                produce(group, begin)
            lax.fori_loop(batch[0], batch[-1] + 1, complete, 0)

    def finish(group, carry):
        send(group).wait()
        return carry

    lax.fori_loop(0, groups, finish, 0)


def body(charge, pad_row, pad_column, time_bin, slab_owner, block_count, shaping, response):
    slabs, pads = lax.axis_size("tm"), lax.axis_size("pad")
    rows = charge.shape[1]
    capacity = max(16, 3 * rows // (2 * slabs))
    room = LANES // 2
    assert capacity <= room and slabs % 2 == 0 and slabs * min(pads, 3) <= 256
    row_count = PROWS // pads
    vmem = pl.BlockSpec(memory_space=pltpu.VMEM)
    chunks = T_DEV // LANES
    sources = (block_count, charge, pad_row, pad_column, time_bin, slab_owner.reshape(1, rows), shaping.reshape(chunks, LANES))
    sources = tuple(pltpu.with_memory_space_constraint(source, pltpu.HBM) for source in sources)
    outgoing, line = pl.pallas_call(
        functools.partial(route_kernel, slabs, pads, row_count, room),
        out_shape=(
            jax.ShapeDtypeStruct((slabs * pads, 4, LANES), jnp.float32),
            jax.ShapeDtypeStruct((chunks, LANES), jnp.float32),
        ),
        in_specs=[pl.BlockSpec(memory_space=pltpu.HBM)] * 7,
        out_specs=(vmem, vmem),
        scratch_shapes=[pltpu.SemaphoreType.DMA((7,)), pltpu.SMEM(block_count.shape, block_count.dtype)]
        + [pltpu.VMEM(source.shape, source.dtype) for source in sources[1:6]],
        compiler_params=pltpu.CompilerParams(vmem_limit_bytes=32 * 2**20),
        name="route",
    )(*sources)
    incoming = lax.all_to_all(outgoing, ("tm", "pad"), split_axis=0, concat_axis=0, tiled=True)

    count = slabs * pads
    step = min(count, 32)
    buckets = -(-(2 * PPR // GROUP + 2) // 8) * 8
    most = -(-slabs * 2 * capacity * min(pads, 3) // SORT) * (SORT // LANES)
    stride = LANES + 4
    signal = pl.pallas_call(
        functools.partial(signal_kernel, row_count),
        out_shape=jax.ShapeDtypeStruct((PPR, row_count, T_DEV), jnp.float32),
        in_specs=[pl.BlockSpec(memory_space=pltpu.HBM), vmem, vmem],
        out_specs=pl.BlockSpec(memory_space=pl.ANY),
        scratch_shapes=[
            pltpu.SMEM(response.shape, response.dtype),
            pltpu.VMEM((count, 16, LANES), jnp.float32),
            pltpu.VMEM((count, 1, LANES), jnp.float32),
            pltpu.VMEM((count * buckets, LANES), jnp.float32),
            pltpu.VMEM((step * buckets, 2 * LANES), jnp.float32),
            pltpu.VMEM((LANES * 3 * chunks, LANES), jnp.float32),
            pltpu.VMEM((most + 1, 4, LANES), jnp.float32),
            pltpu.VMEM((most * LANES // SORT, SORT // LANES, LANES), jnp.int32),
            pltpu.VMEM((buckets, LANES), jnp.int32),
            pltpu.VMEM((2, chunks * stride, LANES), jnp.float32),
            pltpu.VMEM((chunks, most * LANES, LANES), jnp.bfloat16),
            pltpu.VMEM((chunks, most * LANES, LANES), jnp.bfloat16),
            pltpu.VMEM((PPR // GROUP, GROUP * -(-row_count // 8) * 8, 2 * LANES), jnp.bfloat16),
            pltpu.VMEM((PPR, row_count, T_DEV), jnp.float32),
            pltpu.SMEM((most * LANES // SORT, SORT // LANES, LANES), jnp.int32),
            pltpu.SMEM((buckets, LANES), jnp.int32),
            pltpu.SemaphoreType.DMA((2,)),
            pltpu.SemaphoreType.DMA((most * LANES // SORT,)),
            pltpu.SemaphoreType.DMA((PPR // GROUP,)),
        ],
        compiler_params=pltpu.CompilerParams(vmem_limit_bytes=56 * 2**20),
        name="signal",
    )(pltpu.with_memory_space_constraint(response, pltpu.HBM), pltpu.with_memory_space_constraint(incoming, pltpu.VMEM), pltpu.with_memory_space_constraint(line, pltpu.VMEM))
    return signal.transpose(1, 0, 2)


def solution(mesh):
    in_specs = (
        P("pad", "tm"),
        P("pad", "tm"),
        P("pad", "tm"),
        P("pad", "tm"),
        P("pad", "tm", None),
        P("pad", "tm"),
        P(),
        P(),
    )
    out_specs = P("pad", None, "tm")
    return jax.shard_map(body, mesh=mesh, in_specs=in_specs, out_specs=out_specs, check_vma=False)
```
